256 devices in a mesh: box: 64 (over x, z, core), col: 4 (over y).
Axes of the slice: x: 4, y: 4, z: 8, core: 2. Of those that a mesh axis runs over, the one named last changes fastest.
Arguments:
- leaf_maps: float32 [64, 1024, 1024], P('box', None, 'col'), may hold values from -0.08385255 to 0.08385255
- interface_blocks: int32 [3, 64, 4], replicated, may hold values from 0 to 7, as said below
- root_data: float32 [8, 1024, 512], P(None, None, 'col'), may hold values from -6 to 6
Outputs:
- leaf_data: float32 [64, 1024, 512], P('box', None, 'col')
The draws below stay inside these ranges and needn't reach their ends.
Inputs may be any that keep to these rules, and one draw needn't show every extreme that they name: `interface_blocks`: entry k of every list is block 2k or 2k+1.
All inputs are finite; a program needn't handle non-finite values.
Results may differ from the reference program's by a relative error of at most 0.0003.
Values sent between devices are 32-bit elements; how exact they have to be, the bound alone decides.
A program may use at most 128 MiB of HBM per device.

```python
import jax
import jax.numpy as jnp
from jax import lax

NMAP = 1024
BLK = 128
LEVELS = 3
NEWTON = 2
NRHS = 512
IFACE = 512
BLOCKS = 8
BOXES = 64
ROOTS = 8


def draw_leaf_maps(key, part):
    spread = (5 * NMAP // 4) ** (-0.5)
    values = spread * jax.random.truncated_normal(key, -3.0, 3.0, (BOXES, NMAP, NMAP), jnp.float32)
    return values


def draw_interface_blocks(key, part):
    picks = jax.random.randint(key, (LEVELS, BOXES, BLOCKS // 2), 0, 2, dtype=jnp.int32)
    picks = picks.at[0, 0, 0].set(0).at[0, 0, BLOCKS // 2 - 1].set(1)
    offsets = 2 * jnp.arange(BLOCKS // 2, dtype=jnp.int32)
    return offsets[None, None, :] + picks


def steps_of(own_key, shape, shards, least, top_value):
    factor_of = 1.0
    for dim, shards_of in shards:
        draws = jax.random.uniform(jax.random.fold_in(jax.random.fold_in(own_key, 6), dim), (shards_of,), jnp.float32, least / len(shards), top_value / len(shards))
        factor_of = factor_of * jnp.repeat(jnp.exp(draws), shape[dim] // shards_of).reshape((-1,) + (1,) * (len(shape) - 1 - dim))
    return factor_of


def scatter_about(key, shape, scale, reach, cuts=(), kind=jnp.bfloat16):
    drawn = jax.random.normal(key, shape, jnp.float32) * scale
    if len(cuts) > 0:
        drawn = steps_of(key, shape, cuts, -0.22, 0.18) * drawn
    return jnp.clip(drawn, min=-reach, max=reach).astype(kind)


def setup_inputs(seed: int = 0) -> dict:
    streams_of = jax.random.split(jax.random.key(seed), 4)
    return {
        "leaf_maps": draw_leaf_maps(jax.random.fold_in(streams_of[3], 71), 0),
        "interface_blocks": draw_interface_blocks(jax.random.fold_in(streams_of[3], 71), 0),
        "root_data": scatter_about(streams_of[2], (ROOTS, NMAP, NRHS), 1.0, 6.0, ((2, 4),), jnp.float32),
    }


def high_dot(left, right):
    return jnp.dot(left, right, precision=lax.Precision.HIGHEST, preferred_element_type=jnp.float32)


def high_tdot(left, right):
    return lax.dot_general(left, right, (((0,), (0,)), ((), ())), precision=lax.Precision.HIGHEST, preferred_element_type=jnp.float32)


def take_blocks(matrix, block_ids, along, block_width):
    if along == 0:
        shaped = matrix.reshape(matrix.shape[0] // block_width, block_width, matrix.shape[1])
        return jnp.take(shaped, block_ids, axis=0).reshape(-1, matrix.shape[1])
    shaped = matrix.reshape(matrix.shape[0], matrix.shape[1] // block_width, block_width)
    return jnp.take(shaped, block_ids, axis=1).reshape(matrix.shape[0], -1)


def merge_operators(alpha_map, beta_map, alpha_list, beta_list):
    offsets = 2 * jnp.arange(alpha_list.shape[0], dtype=jnp.int32)
    alpha_bit = alpha_list - offsets
    beta_bit = beta_list - offsets
    alpha_ext = offsets + 1 - alpha_bit
    beta_ext = offsets + 1 - beta_bit
    alpha_rows = take_blocks(alpha_map, alpha_list, 0, BLK)
    beta_rows = take_blocks(beta_map, beta_list, 0, BLK)
    alpha_inner = take_blocks(alpha_rows, alpha_list, 1, BLK)
    alpha_outer = take_blocks(alpha_rows, alpha_ext, 1, BLK)
    beta_inner = take_blocks(beta_rows, beta_list, 1, BLK)
    beta_outer = take_blocks(beta_rows, beta_ext, 1, BLK)
    identity = jnp.eye(IFACE, dtype=jnp.float32)
    product = high_dot(beta_inner, alpha_inner)
    iterate = identity + product
    defect = identity - product
    for _ in range(NEWTON):
        iterate = 2.0 * iterate - high_dot(iterate, high_dot(defect, iterate))
    return (alpha_inner, beta_inner, iterate, alpha_outer, beta_outer, alpha_bit, beta_bit, alpha_ext, beta_ext)


def merged_map(alpha_map, beta_map, operators):
    alpha_inner, beta_inner, coupling, alpha_outer, beta_outer, alpha_bit, beta_bit, alpha_ext, beta_ext = operators
    coupling_beta = high_dot(coupling, beta_inner)
    alpha_cols = high_dot(coupling_beta, alpha_outer)
    alpha_back = -(alpha_outer + high_dot(alpha_inner, alpha_cols))
    beta_cols = -high_dot(coupling, beta_outer)
    beta_back = -high_dot(alpha_inner, beta_cols)
    alpha_block = take_blocks(take_blocks(alpha_map, alpha_ext, 0, BLK), alpha_ext, 1, BLK)
    beta_block = take_blocks(take_blocks(beta_map, beta_ext, 0, BLK), beta_ext, 1, BLK)
    upper_rows = jnp.concatenate([alpha_block + high_tdot(alpha_outer, alpha_cols), high_tdot(alpha_outer, beta_cols)], 1)
    lower_rows = jnp.concatenate([high_tdot(beta_outer, alpha_back), beta_block + high_tdot(beta_outer, beta_back)], 1)
    assembled = jnp.concatenate([upper_rows, lower_rows], 0)
    pairs_count = IFACE // BLK
    assembled = assembled.reshape(2, pairs_count, BLK, 2, pairs_count, BLK).transpose(1, 0, 2, 4, 3, 5)
    return assembled.reshape(NMAP, NMAP)


def place_blocks(far_data, near_data, bits):
    pairs_count = bits.shape[0]
    columns = far_data.shape[1]
    chooser = bits[:, None] == jnp.arange(2, dtype=jnp.int32)[None, :]
    shaped_far = far_data.reshape(pairs_count, 1, BLK, columns)
    shaped_near = near_data.reshape(pairs_count, 1, BLK, columns)
    return jnp.where(chooser[:, :, None, None], shaped_near, shaped_far).reshape(pairs_count * 2 * BLK, columns)


def descend(parent, operators):
    alpha_inner, beta_inner, coupling, alpha_outer, beta_outer, alpha_bit, beta_bit, alpha_ext, beta_ext = operators
    columns = parent.shape[1]
    split_rows = parent.reshape(alpha_bit.shape[0], 2, BLK, columns)
    alpha_far = split_rows[:, 0].reshape(-1, columns)
    beta_far = split_rows[:, 1].reshape(-1, columns)
    through = high_dot(alpha_outer, alpha_far)
    alpha_near = high_dot(coupling, high_dot(beta_inner, through) - high_dot(beta_outer, beta_far))
    beta_near = -(through + high_dot(alpha_inner, alpha_near))
    return place_blocks(alpha_far, alpha_near, alpha_bit), place_blocks(beta_far, beta_near, beta_bit)


def reference(leaf_maps, interface_blocks, root_data):
    current = leaf_maps
    stored = []
    for level_index in range(LEVELS):
        span = 2 ** level_index
        alpha_lists = interface_blocks[level_index, 0::2 * span]
        beta_lists = interface_blocks[level_index, span::2 * span]
        alpha_maps = current[0::2]
        beta_maps = current[1::2]
        operators = jax.vmap(merge_operators)(alpha_maps, beta_maps, alpha_lists, beta_lists)
        stored.append(operators)
        if level_index + 1 < LEVELS:
            current = jax.vmap(merged_map)(alpha_maps, beta_maps, operators)
    data = root_data
    for level_index in reversed(range(LEVELS)):
        alpha_data, beta_data = jax.vmap(descend)(data, stored[level_index])
        data = jnp.stack([alpha_data, beta_data], 1).reshape(-1, NMAP, NRHS)
    return data
```

```python
import functools

import jax
import jax.numpy as jnp
from jax import lax
from jax.experimental import pallas as pl
from jax.experimental.pallas import tpu as pltpu
from jax.sharding import PartitionSpec as P

LEVELS = 3
IFACE = 512
BLK = 128
HALF = 256
F32 = jnp.float32
BF16 = jnp.bfloat16
MESH = pl.DeviceIdType.MESH

ACROSS, RIGHT, LEFT, ON_RIGHT, ON_LEFT, SIBLING, COPIES = 0, 1, 3, 5, 6, 7, 15


def split(x):
    high = x.astype(BF16)
    return high, (x - high.astype(F32)).astype(BF16)


def mm(a, b):
    dot = functools.partial(jnp.dot, preferred_element_type=F32)
    return dot(a[0], b[0]) + (dot(a[0], b[1]) + dot(a[1], b[0]))


def pick(flag, yes, no):
    return jnp.where(jnp.broadcast_to(flag, yes.shape) == 1, yes, no)


def kernel(
    table, leaf, root, out,
    g0i, g0o, g1i, g1o, g2i, g2o,
    mats, work, wf, vs, ss, ext, dall, p, fs, t32, ts, ds,
    send_sem, recv_sem, ext_send, ext_recv, root_sem,
):
    pos = lax.axis_index("box")
    y = lax.axis_index("col")
    c = pos % 2
    gathered = ((g0i, g0o), (g1i, g1o), (g2i, g2o))
    slots = (y, (y + 3) % 4, (y + 1) % 4, (y + 2) % 4)
    right, left, sibling = (pos, slots[2]), (pos, slots[1]), (pos ^ 1, y)

    root_copy = pltpu.make_async_copy(root.at[pos // 8], p, root_sem)
    root_copy.start()

    barrier = pltpu.get_barrier_semaphore()
    for peer in (right, left, sibling, (pos ^ 2, y), (pos ^ 4, y)):
        pl.semaphore_signal(barrier, inc=1, device_id=peer, device_id_type=MESH)

    def own_map(level):
        return (pos >> level) & 1

    def bit_of(level, k):
        return table[level, pos - pos % 2**level, k] & 1

    def unit(level, phase, slot, u):
        g = gathered[level][phase]
        return g.at[slot, c, u] if level == 0 else g.at[slot, u, c]

    def other_unit(level, phase, slot, u):
        g = gathered[level][phase]
        return g.at[slot, 1 - c, u] if level == 0 else g.at[slot, u, 1 - c]

    def copy(level, phase, ref, index, peer):
        return pltpu.make_async_remote_copy(
            src_ref=ref,
            dst_ref=ref,
            send_sem=send_sem.at[level, phase, index],
            recv_sem=recv_sem.at[level, phase, index],
            device_id=peer,
            device_id_type=MESH,
        )

    def send(*args):
        copy(*args).start()

    def to_sibling(level, phase, rel, u):
        send(level, phase, unit(level, phase, slots[rel], u), SIBLING + 2 * rel + u, sibling)

    def send_unit(level, phase, u):
        ref = unit(level, phase, y, u)
        send(level, phase, ref, RIGHT + u, right)
        send(level, phase, ref, LEFT + u, left)
        to_sibling(level, phase, 0, u)

    def start(level, phase):
        if level == 0:
            first, second = unit(0, phase, y, 0), unit(0, phase, y, 1)
            send(0, phase, first, RIGHT, right)
            send(0, phase, second, LEFT + 1, left)
            send(0, phase, second, RIGHT + 1, right)
            send(0, phase, first, LEFT, left)
            to_sibling(0, phase, 0, 0)
            to_sibling(0, phase, 0, 1)
        else:
            mine = own_map(level)
            send(level, phase, unit(level, phase, y, mine), ACROSS, (pos ^ 2**level, y))
            send_unit(level, phase, mine)

    def across(level, phase):
        if level:
            theirs = 1 - own_map(level)
            ref = unit(level, phase, y, theirs)
            copy(level, phase, ref, ACROSS, (pos ^ 2**level, y)).wait_recv()
            send_unit(level, phase, theirs)

    def arrived(level, phase, rel, u, index):
        copy(level, phase, unit(level, phase, slots[rel], u), index, left).wait_recv()

    def forward(level, phase):
        arrived(level, phase, 1, 0, RIGHT)
        send(level, phase, unit(level, phase, slots[1], 0), ON_RIGHT, right)
        to_sibling(level, phase, 1, 0)
        arrived(level, phase, 2, 1, LEFT + 1)
        send(level, phase, unit(level, phase, slots[2], 1), ON_LEFT, left)
        to_sibling(level, phase, 2, 1)

    def near_rest(level, phase):
        arrived(level, phase, 1, 1, RIGHT + 1)
        to_sibling(level, phase, 1, 1)
        arrived(level, phase, 2, 0, LEFT)
        to_sibling(level, phase, 2, 0)

    def far(level, phase):
        arrived(level, phase, 3, 0, ON_RIGHT)
        to_sibling(level, phase, 3, 0)
        arrived(level, phase, 3, 1, ON_LEFT)
        to_sibling(level, phase, 3, 1)

    def convert(level, phase, rel):
        for u in range(2):
            ref = other_unit(level, phase, slots[rel], u)
            copy(level, phase, ref, SIBLING + 2 * rel + u, sibling).wait_recv()
        columns = pl.ds(pl.multiple_of(slots[rel] * BLK, BLK), BLK)
        g = gathered[level][phase]
        for m in range(2):
            for r in range(2):
                high, low = split(g[slots[rel], m, r])
                mats[level, 2 * phase + m, 0, r * HALF : (r + 1) * HALF, columns] = high
                mats[level, 2 * phase + m, 1, r * HALF : (r + 1) * HALF, columns] = low

    def rows_of(i):
        return pl.ds(pl.multiple_of(i * HALF, HALF), HALF)

    def product(a, b, finish):
        def half(i, carry):
            rows = rows_of(i)
            finish(rows, mm((a[0, rows, :], a[1, rows, :]), (b[0], b[1])))
            return carry

        lax.fori_loop(0, 2, half, 0)

    def keep(ref, rows, x):
        high, low = split(x)
        ref[0, rows, :] = high
        ref[1, rows, :] = low

    bit_y = bit_of(0, y)
    for k in range(4):
        bit = bit_of(0, k)
        even = leaf[0, 2 * k * BLK : (2 * k + 1) * BLK, :]
        odd = leaf[0, (2 * k + 1) * BLK : (2 * k + 2) * BLK, :]
        rows = slice(k % 2 * BLK, (k % 2 + 1) * BLK)
        near = pick(bit, odd, even)
        away = pick(bit, even, odd)
        g0i[y, c, k // 2, rows, :] = pick(bit_y, near[:, BLK:], near[:, :BLK])
        g0o[y, c, k // 2, rows, :] = pick(bit_y, near[:, :BLK], near[:, BLK:])
        dall[k // 2, rows, :] = pick(bit_y, away[:, :BLK], away[:, BLK:])
    ext[0, c] = dall[c]

    pl.semaphore_wait(barrier, 5)

    def ext_copy(level):
        return pltpu.make_async_remote_copy(
            src_ref=dall.at[1 - c] if level == 0 else ext.at[1, own_map(1)],
            dst_ref=ext.at[level, own_map(level)],
            send_sem=ext_send.at[level],
            recv_sem=ext_recv.at[level],
            device_id=(pos ^ 2**level, y),
            device_id_type=MESH,
        )

    for level in range(LEVELS):
        start(level, 0)
        across(level, 0)
        convert(level, 0, 0)
        forward(level, 0)
        near_rest(level, 0)
        start(level, 1)
        convert(level, 0, 1)
        convert(level, 0, 2)
        far(level, 0)
        if level < 2:
            ext_copy(level).start()
        convert(level, 0, 3)
        across(level, 1)

        alpha, beta, alpha_out, beta_out, coupling = (mats.at[level, i] for i in range(5))
        one, two, four, three = (work.at[i] for i in range(4))

        def first(rows, x):
            wf[0, rows, :] = x
            keep(one, rows, x)

        product(beta, alpha, first)

        def second(rows, x):
            wf[1, rows, :] = x
            keep(two, rows, x)

        product(one, one, second)
        forward(level, 1)

        def third(rows, x):
            shape = x.shape
            row = lax.broadcasted_iota(jnp.int32, shape, 0) + rows.start
            column = lax.broadcasted_iota(jnp.int32, shape, 1)
            x = x + wf[0, rows, :] + wf[1, rows, :] + jnp.where(row == column, 1.0, 0.0)
            wf[0, rows, :] = x
            keep(three, rows, x)

        product(one, two, third)
        near_rest(level, 1)
        product(two, two, lambda rows, x: keep(four, rows, x))
        convert(level, 1, 0)
        product(three, four, lambda rows, x: keep(coupling, rows, wf[0, rows, :] + x))

        if level < 2:
            mine = pl.ds(pl.multiple_of(y * BLK, BLK), BLK)

            def couple(i, carry):
                rows = rows_of(i)
                x = mm(
                    (beta[0, rows, :], beta[1, rows, :]),
                    (alpha_out[0, :, mine], alpha_out[1, :, mine]),
                )
                high, low = split(x)
                vs[0, rows, :BLK] = high
                vs[1, rows, :BLK] = low
                vs[0, rows, BLK:] = -beta_out[0, rows, mine]
                vs[1, rows, BLK:] = -beta_out[1, rows, mine]
                return carry

            lax.fori_loop(0, 2, couple, 0)
            far(level, 1)
            product(coupling, vs, lambda rows, x: keep(ss.at[0], rows, x))

            def back(i, carry):
                rows = rows_of(i)
                x = -mm((alpha[0, rows, :], alpha[1, rows, :]), (ss[0, 0], ss[0, 1]))
                own = gathered[level][1][y, 0, i]
                x = jnp.concatenate([x[:, :BLK] - own, x[:, BLK:]], 1)
                keep(ss.at[1], rows, x)
                return carry

            lax.fori_loop(0, 2, back, 0)
        else:
            far(level, 1)
        convert(level, 1, 1)
        convert(level, 1, 2)
        convert(level, 1, 3)

        if level < 2:
            ext_copy(level).wait_recv()
            above = level + 1
            bit_y = bit_of(above, y)
            outer = gathered[level][1]

            def merged(kk, chosen):
                k = 2 * c + kk
                bit = bit_of(above, k)
                part = bit if chosen else 1 - bit
                r = pick(part, outer[k, 1], outer[k, 0]).reshape(IFACE, BLK)
                x = mm(split(r.T), (ss[part, 0], ss[part, 1]))
                rows = slice(kk * BLK, (kk + 1) * BLK)
                kept = pick(part, ext[level, 1, rows, :], ext[level, 0, rows, :])
                return x[:, :BLK], x[:, BLK:], kept, part, rows

            for kk in range(2):
                lower, upper, kept, part, rows = merged(kk, True)
                lower = lower + pick(part, jnp.zeros_like(kept), kept)
                upper = upper + pick(part, kept, jnp.zeros_like(kept))
                gi, go = gathered[above]
                gi[y, own_map(above), c, rows, :] = pick(bit_y, upper, lower)
                go[y, own_map(above), c, rows, :] = pick(bit_y, lower, upper)
            if level == 0:
                for kk in range(2):
                    lower, upper, kept, part, rows = merged(kk, False)
                    lower = lower + pick(part, jnp.zeros_like(kept), kept)
                    upper = upper + pick(part, kept, jnp.zeros_like(kept))
                    ext[1, own_map(1), rows, :] = pick(bit_y, lower, upper)

    root_copy.wait()
    for level in reversed(range(LEVELS)):
        alpha, beta, alpha_out, beta_out, coupling = (mats.at[level, i] for i in range(5))
        for k in range(4):
            rows = slice(k * BLK, (k + 1) * BLK)
            keep(fs.at[0], rows, p[2 * k * BLK : (2 * k + 1) * BLK, :])
            keep(fs.at[1], rows, p[(2 * k + 1) * BLK : (2 * k + 2) * BLK, :])

        def through(rows, x):
            t32[0, rows, :] = x
            keep(ts, rows, x)

        product(alpha_out, fs.at[0], through)

        def feed(i, carry):
            rows = rows_of(i)
            x = mm((beta[0, rows, :], beta[1, rows, :]), (ts[0], ts[1]))
            x = x - mm((beta_out[0, rows, :], beta_out[1, rows, :]), (fs[1, 0], fs[1, 1]))
            keep(ds, rows, x)
            return carry

        lax.fori_loop(0, 2, feed, 0)

        def solve(rows, x):
            t32[1, rows, :] = x
            keep(ts, rows, x)

        product(coupling, ds, solve)

        upper_half = own_map(level)

        def close(rows, x):
            fb = -(t32[0, rows, :] + x)
            t32[0, rows, :] = pick(upper_half, fb, t32[1, rows, :])

        product(alpha, ts, close)
        target = p if level else out.at[0]
        for k in range(4):
            bit = bit_of(level, k)
            near = t32[0, k * BLK : (k + 1) * BLK, :]
            f1 = p[2 * k * BLK : (2 * k + 1) * BLK, :]
            f2 = p[(2 * k + 1) * BLK : (2 * k + 2) * BLK, :]
            away = pick(upper_half, f2, f1)
            target[2 * k * BLK : (2 * k + 1) * BLK, :] = pick(bit, away, near)
            target[(2 * k + 1) * BLK : (2 * k + 2) * BLK, :] = pick(bit, near, away)

    for level in range(LEVELS):
        for phase in range(2):
            if level:
                ref = unit(level, phase, y, own_map(level))
                copy(level, phase, ref, ACROSS, left).wait_send()
            for index in range(1, COPIES):
                copy(level, phase, unit(level, phase, y, 0), index, left).wait_send()
    for level in range(2):
        ext_copy(level).wait_send()


def shards(leaf_maps, interface_blocks, root_data):
    vmem = pl.BlockSpec(memory_space=pltpu.VMEM)
    units = pltpu.VMEM((4, 2, 2, HALF, BLK), F32)
    return pl.pallas_call(
        kernel,
        out_shape=jax.ShapeDtypeStruct((1,) + root_data.shape[1:], F32),
        in_specs=[
            pl.BlockSpec(memory_space=pltpu.SMEM),
            vmem,
            pl.BlockSpec(memory_space=pl.ANY),
        ],
        out_specs=vmem,
        scratch_shapes=[units] * 6
        + [
            pltpu.VMEM((LEVELS, 5, 2, IFACE, IFACE), BF16),
            pltpu.VMEM((4, 2, IFACE, IFACE), BF16),
            pltpu.VMEM((2, IFACE, IFACE), F32),
            pltpu.VMEM((2, IFACE, HALF), BF16),
            pltpu.VMEM((2, 2, IFACE, HALF), BF16),
            pltpu.VMEM((2, 2, HALF, BLK), F32),
            pltpu.VMEM((2, HALF, BLK), F32),
            pltpu.VMEM((2 * IFACE, BLK), F32),
            pltpu.VMEM((2, 2, IFACE, BLK), BF16),
            pltpu.VMEM((2, IFACE, BLK), F32),
            pltpu.VMEM((2, IFACE, BLK), BF16),
            pltpu.VMEM((2, IFACE, BLK), BF16),
            pltpu.SemaphoreType.DMA((LEVELS, 2, COPIES)),
            pltpu.SemaphoreType.DMA((LEVELS, 2, COPIES)),
            pltpu.SemaphoreType.DMA((2,)),
            pltpu.SemaphoreType.DMA((2,)),
            pltpu.SemaphoreType.DMA,
        ],
        compiler_params=pltpu.CompilerParams(
            collective_id=0, has_side_effects=True, vmem_limit_bytes=56 * 2**20
        ),
        name="merge_and_sweep",
    )(interface_blocks, leaf_maps, root_data)


def solution(mesh):
    return jax.shard_map(
        shards,
        mesh=mesh,
        in_specs=(P("box", None, "col"), P(), P(None, None, "col")),
        out_specs=P("box", None, "col"),
        check_vma=False,
    )
```

```python
import functools

import jax
import jax.numpy as jnp
from jax import lax
from jax.experimental import pallas as pl
from jax.experimental.pallas import tpu as pltpu
from jax.sharding import PartitionSpec as P

LEVELS = 3
IFACE = 512
BLK = 128
HALF = 256
F32 = jnp.float32
BF16 = jnp.bfloat16
MESH = pl.DeviceIdType.MESH

ACROSS, RIGHT, LEFT, FAR, SIBLING, BESIDE, COPIES = 0, 1, 3, 5, 7, 15, 23


def split(x):
    high = x.astype(BF16)
    return high, (x - high.astype(F32)).astype(BF16)


def mm(a, b):
    dot = functools.partial(jnp.dot, preferred_element_type=F32)
    return dot(a[0], b[0]) + (dot(a[0], b[1]) + dot(a[1], b[0]))


def pick(flag, yes, no):
    return jnp.where(jnp.broadcast_to(flag, yes.shape) == 1, yes, no)


def kernel(
    table, leaf, root, out,
    g0i, g0o, g1i, g1o, g2i, g2o,
    raw, both, down, mats, work, wf, vs, vf, ss, ext, dall, p, fs, t32, ts, ds,
    send_sem, recv_sem, ext_send, ext_recv, root_sem,
):
    pos = lax.axis_index("box")
    y = lax.axis_index("col")
    c = pos % 2
    gathered = ((g0i, g0o), (g1i, g1o), (g2i, g2o))
    slots = (y, (y + 3) % 4, (y + 1) % 4, (y + 2) % 4)
    right, left, opposite, sibling = (pos, slots[2]), (pos, slots[1]), (pos, slots[3]), (pos ^ 1, y)

    root_copy = pltpu.make_async_copy(root.at[pos // 8], p, root_sem)
    root_copy.start()

    barrier = pltpu.get_barrier_semaphore()
    for peer in (right, left, opposite, sibling, (pos ^ 2, y), (pos ^ 4, y)):
        pl.semaphore_signal(barrier, inc=1, device_id=peer, device_id_type=MESH)

    def own_map(level):
        return (pos >> level) & 1

    def bit_of(level, k):
        return table[level, pos - pos % 2**level, k] & 1

    def next_bit(level, k):
        return bit_of(level + 1, k) if level + 1 < LEVELS else jnp.int32(0)

    def unit(level, phase, slot, u):
        g = gathered[level][phase]
        return g.at[slot, c, u] if level + phase == 0 else g.at[slot, u, c]

    def copy(level, phase, ref, index, peer, src=None):
        return pltpu.make_async_remote_copy(
            src_ref=ref if src is None else src,
            dst_ref=ref,
            send_sem=send_sem.at[level, phase, index],
            recv_sem=recv_sem.at[level, phase, index],
            device_id=peer,
            device_id_type=MESH,
        )

    def send(*args):
        copy(*args).start()

    z_low = (pos >> 1) & 1
    beside = (pos ^ 2, y)

    def half(ref, which):
        return ref.at[pl.ds(pl.multiple_of(which * BLK, BLK), BLK)]

    def to_beside(level, phase, rel, u):
        ref = half(unit(level, phase, slots[rel], u), z_low)
        send(level, phase, ref, BESIDE + 2 * rel + u, beside)

    def split_around(level, phase, u):
        ref = half(unit(level, phase, y, u), z_low)
        send(level, phase, ref, RIGHT + u, right)
        send(level, phase, ref, LEFT + u, left)
        send(level, phase, ref, FAR + u, opposite)

    def serve_split(level, phase, u):
        for rel in (1, 2, 3):
            ref = half(unit(level, phase, slots[rel], u), z_low)
            copy(level, phase, ref, (0, RIGHT, LEFT, FAR)[rel] + u, left).wait_recv()
            to_beside(level, phase, rel, u)

    def join_split(level, phase, u, rels=(1, 2, 3)):
        for rel in rels:
            ref = half(unit(level, phase, slots[rel], u), 1 - z_low)
            copy(level, phase, ref, BESIDE + 2 * rel + u, beside).wait_recv()
            to_sibling(level, phase, rel, u)

    def to_sibling(level, phase, rel, u):
        send(level, phase, unit(level, phase, slots[rel], u), SIBLING + 2 * rel + u, sibling)

    def from_sibling(level, phase, rel, u):
        ref = unit(level, phase, slots[rel], u)
        copy(level, phase, ref, SIBLING + 2 * rel + u, sibling).wait_recv()

    def send_next(level, phase, u):
        ref = unit(level, phase, y, u)
        send(level, phase, ref, RIGHT + u, right)
        send(level, phase, ref, LEFT + u, left)

    def send_far(level, phase, u):
        send(level, phase, unit(level, phase, y, u), FAR + u, opposite)

    def send_around(level, phase, u):
        send_next(level, phase, u)
        send_far(level, phase, u)

    def sent(level, phase, u, kinds):
        ref = unit(level, phase, y, u)
        for index in kinds:
            copy(level, phase, ref, index + u, right).wait_send()

    def arrived(level, phase, rel, u):
        index = (0, RIGHT, LEFT, FAR)[rel] + u
        copy(level, phase, unit(level, phase, slots[rel], u), index, left).wait_recv()

    def relay_far(level):
        mine = own_map(level)
        ref = unit(level, 0, slots[3], mine)
        pltpu.make_async_remote_copy(
            src_ref=ref,
            dst_ref=ref,
            send_sem=send_sem.at[level, 0, FAR + 1 - mine],
            recv_sem=recv_sem.at[level, 0, FAR + mine],
            device_id=(pos ^ 2**level, y),
            device_id_type=MESH,
        ).start()

    def serve(level, phase, u, rels=(1, 2, 3)):
        for rel in rels:
            arrived(level, phase, rel, u)
            to_sibling(level, phase, rel, u)

    def columns_of(rel):
        return pl.ds(pl.multiple_of(slots[rel] * BLK, BLK), BLK)

    def rows_of(i):
        return pl.ds(pl.multiple_of(i * HALF, HALF), HALF)

    def keep(ref, rows, x, columns=slice(None)):
        high, low = split(x)
        ref[0, rows, columns] = high
        ref[1, rows, columns] = low

    def keep_inner(level, rel, m):
        for r in range(2):
            x = gathered[level][0][slots[rel], m, r]
            keep(mats.at[level, m], slice(r * HALF, (r + 1) * HALF), x, columns_of(rel))

    def keep_outer(level, rel, awaited=(0, 1)):
        for q in awaited:
            from_sibling(level, 1, rel, q)
        bit = next_bit(level, slots[rel])
        g = gathered[level][1]
        for r in range(2):
            rows = slice(r * HALF, (r + 1) * HALF)
            chosen, rest = g[slots[rel], 0, r], g[slots[rel], 1, r]
            keep(mats.at[level, 2], rows, pick(bit, rest, chosen), columns_of(rel))
            keep(mats.at[level, 3], rows, pick(bit, chosen, rest), columns_of(rel))

    def pair(ref):
        return ref[0], ref[1]

    everything = slice(None)

    def order_outer(level):
        theirs = 1 - own_map(level)
        copy(level, 1, raw.at[level, theirs], ACROSS, sibling).wait_recv()
        bit = next_bit(level, y)
        g = gathered[level][1]
        g[y, 0, c] = pick(bit, raw[level, 1], raw[level, 0])
        g[y, 1, c] = pick(bit, raw[level, 0], raw[level, 1])
        to_sibling(level, 1, 0, 0)
        to_sibling(level, 1, 0, 1)

    def finish_cubes(level):
        one, two, four, three = (work.at[i] for i in range(4))
        x = mm(pair(one), pair(two)) + wf[0] + wf[1]
        row = lax.broadcasted_iota(jnp.int32, x.shape, 0)
        column = lax.broadcasted_iota(jnp.int32, x.shape, 1)
        x = x + jnp.where(row == column, 1.0, 0.0)
        wf[0] = x
        keep(three, everything, x)
        keep(four, everything, mm(pair(two), pair(two)))

    def finish_coupling(level):
        keep(mats.at[level, 4], everything, wf[0] + mm(pair(work.at[3]), pair(work.at[2])))

    def sweep_operator(level):
        alpha, beta, alpha_out, beta_out, coupling = (mats.at[level, i] for i in range(5))
        x = mm(pair(beta), pair(alpha_out))
        keep(work.at[0], everything, x)
        keep(work.at[1], everything, mm(pair(coupling), pair(work.at[0])))
        keep(work.at[2], everything, -mm(pair(coupling), pair(beta_out)))
        upper_half = own_map(level)
        for i in range(2):
            near = work.at[1 + i]
            x = -mm(pair(alpha), pair(near))
            if i == 0:
                x = x - (alpha_out[0].astype(F32) + alpha_out[1].astype(F32))
            held = near[0].astype(F32) + near[1].astype(F32)
            columns = slice(i * IFACE, (i + 1) * IFACE)
            keep(down.at[level], everything, pick(upper_half, x, held), columns)

    def ext_copy(level):
        return pltpu.make_async_remote_copy(
            src_ref=dall.at[1 - c] if level == 0 else ext.at[1, own_map(1)],
            dst_ref=ext.at[level, own_map(level)],
            send_sem=ext_send.at[level],
            recv_sem=ext_recv.at[level],
            device_id=(pos ^ 2**level, y),
            device_id_type=MESH,
        )

    def merged(level, kk, rest):
        k = 2 * c + kk
        bit = bit_of(level + 1, k)
        part = 1 - bit if rest else bit
        r = gathered[level][1][k, rest].reshape(IFACE, BLK)
        x = mm(split(r.T), (ss[part, 0], ss[part, 1]))
        rows = slice(kk * BLK, (kk + 1) * BLK)
        kept = pick(part, ext[level, 1, rows, :], ext[level, 0, rows, :])
        lower = x[:, :BLK] + pick(part, jnp.zeros_like(kept), kept)
        upper = x[:, BLK:] + pick(part, kept, jnp.zeros_like(kept))
        return lower, upper, rows

    bit_y = bit_of(0, y)
    for k in range(4):
        bit = bit_of(0, k)
        even = leaf[0, 2 * k * BLK : (2 * k + 1) * BLK, :]
        odd = leaf[0, (2 * k + 1) * BLK : (2 * k + 2) * BLK, :]
        rows = slice(k % 2 * BLK, (k % 2 + 1) * BLK)
        near = pick(bit, odd, even)
        away = pick(bit, even, odd)
        g0i[y, c, k // 2, rows, :] = pick(bit_y, near[:, BLK:], near[:, :BLK])
        both[k // 2, rows, :] = pick(bit_y, near[:, :BLK], near[:, BLK:])
        dall[k // 2, rows, :] = pick(bit_y, away[:, :BLK], away[:, BLK:])

    pl.semaphore_wait(barrier, 6)

    for level in range(LEVELS):
        alpha, beta, alpha_out, beta_out, coupling = (mats.at[level, i] for i in range(5))
        one, two, four, three = (work.at[i] for i in range(4))
        mine = own_map(level)
        if level == 0:
            first, second = unit(0, 0, y, 0), unit(0, 0, y, 1)
            send(0, 0, first, RIGHT, right)
            send(0, 0, second, LEFT + 1, left)
            send(0, 0, second, RIGHT + 1, right)
            send(0, 0, first, LEFT, left)
            to_sibling(0, 0, 0, 0)
            to_sibling(0, 0, 0, 1)
            send(0, 1, raw.at[0, mine], ACROSS, sibling, both.at[1 - c])
            ext_copy(0).start()
            raw[0, mine] = both[c]
            ext[0, mine] = dall[c]
            order_outer(0)
            for u in range(2):
                from_sibling(0, 0, 0, u)
            keep_inner(0, 0, 0)
            keep_inner(0, 0, 1)
            arrived(0, 0, 1, 0)
            send(0, 0, unit(0, 0, slots[1], 0), FAR, right)
            to_sibling(0, 0, 1, 0)
            arrived(0, 0, 2, 1)
            send(0, 0, unit(0, 0, slots[2], 1), FAR + 1, left)
            to_sibling(0, 0, 2, 1)
            keep_outer(0, 0)
            arrived(0, 0, 1, 1)
            to_sibling(0, 0, 1, 1)
            arrived(0, 0, 2, 0)
            to_sibling(0, 0, 2, 0)
            send_around(0, 1, 0)
            for rel in (1, 2):
                for u in range(2):
                    from_sibling(0, 0, rel, u)
                keep_inner(0, rel, 0)
                keep_inner(0, rel, 1)
            for u in range(2):
                arrived(0, 0, 3, u)
                to_sibling(0, 0, 3, u)
            for u in range(2):
                from_sibling(0, 0, 3, u)
            keep_inner(0, 3, 0)
            keep_inner(0, 3, 1)
        else:
            theirs = 1 - mine
            last = level == LEVELS - 1
            partner = (pos ^ 2**level, y)
            if last:
                send(level, 0, half(unit(level, 0, y, mine), z_low), ACROSS, partner)
                split_around(level, 0, mine)
                to_sibling(level, 0, 0, mine)
                send(level, 1, unit(level, 1, y, mine), ACROSS, partner)
                to_sibling(level, 1, 0, mine)
                finish_cubes(level - 1)
                serve_split(level - 1, 1, 1)
                send_next(level, 1, mine)
                ref = half(unit(level, 0, y, theirs), z_low)
                copy(level, 0, ref, ACROSS, partner).wait_recv()
                split_around(level, 0, theirs)
                to_beside(level, 0, 0, theirs)
                serve_split(level, 0, mine)
                finish_coupling(level - 1)
                join_split(level - 1, 1, 1)
                join_split(level, 0, theirs, (0,))
                for rel in range(1, 4):
                    keep_outer(level - 1, rel, (1,))
                send_far(level, 1, mine)
                join_split(level, 0, mine)
                serve_split(level, 0, theirs)
                copy(level, 1, unit(level, 1, y, theirs), ACROSS, partner).wait_recv()
                to_sibling(level, 1, 0, theirs)
                send_around(level, 1, theirs)
                for rel in range(4):
                    from_sibling(level, 0, rel, mine)
                    keep_inner(level, rel, mine)
                keep_outer(level, 0)
                sweep_operator(1)
                join_split(level, 0, theirs)
                for rel in range(4):
                    from_sibling(level, 0, rel, theirs)
                    keep_inner(level, rel, theirs)
            else:
                send(level, 0, unit(level, 0, y, mine), ACROSS, partner)
                send_around(level, 0, mine)
                to_sibling(level, 0, 0, mine)
                send(level, 1, raw.at[level, mine], ACROSS, partner)
                finish_cubes(level - 1)
                copy(level, 0, unit(level, 0, y, theirs), ACROSS, partner).wait_recv()
                send_next(level, 0, theirs)
                to_sibling(level, 0, 0, theirs)
                order_outer(level)
                serve(level - 1, 1, 1)
                serve(level, 0, mine)
                relay_far(level)
                finish_coupling(level - 1)
                for rel in range(1, 4):
                    keep_outer(level - 1, rel, (1,))
                bit_y = bit_of(1, y)
                for kk in range(2):
                    lower, upper, rows = merged(0, kk, 1)
                    ext[1, mine, rows, :] = pick(bit_y, lower, upper)
                ext_copy(1).start()
                sent(level, 0, theirs, (RIGHT, LEFT))
                send_around(level, 1, 0)
                for rel in range(4):
                    from_sibling(level, 0, rel, mine)
                    keep_inner(level, rel, mine)
                keep_outer(level, 0)
                serve(level, 0, theirs, (1, 2))
                sweep_operator(0)
                for rel in range(3):
                    from_sibling(level, 0, rel, theirs)
                    keep_inner(level, rel, theirs)
                serve(level, 0, theirs, (3,))
                from_sibling(level, 0, 3, theirs)
                keep_inner(level, 3, theirs)

        if level == LEVELS - 1:
            x = mm(pair(beta), pair(alpha))
            wf[0] = x
            keep(one, everything, x)
            serve(level, 1, mine)
            x = mm(pair(one), pair(one))
            wf[1] = x
            keep(two, everything, x)
            finish_cubes(level)
            finish_coupling(level)
            serve(level, 1, theirs)
            for rel in range(1, 4):
                keep_outer(level, rel)
            break

        own = columns_of(0)
        bit = next_bit(level, y)
        x = mm(
            pair(beta),
            [jnp.concatenate([alpha[i], alpha_out[i, :, own]], 1) for i in range(2)],
        )
        wf[0] = x[:, :IFACE]
        keep(one, everything, x[:, :IFACE])
        vf[:, :BLK] = x[:, IFACE:]
        for r in range(2):
            chosen, rest = gathered[level][1][y, 0, r], gathered[level][1][y, 1, r]
            vf[r * HALF : (r + 1) * HALF, BLK:] = -pick(bit, chosen, rest)
        keep(vs, everything, vf[...])
        x = mm(pair(one), [jnp.concatenate([one[i], vs[i]], 1) for i in range(2)])
        wf[1] = x[:, :IFACE]
        keep(two, everything, x[:, :IFACE])
        x = vf[...] + x[:, IFACE:]
        vf[...] = x
        keep(vs, everything, x)
        (send_around if level == 0 else split_around)(level, 1, 1)
        x = vf[...] + mm(pair(two), pair(vs))
        vf[...] = x
        keep(vs, everything, x)
        keep(vs, everything, mm(pair(two), pair(vs)))
        serve(level, 1, 0)
        x = vf[...] + mm(pair(two), pair(vs))
        keep(ss.at[0], everything, x)
        x = -mm(pair(alpha), pair(ss.at[0]))
        for r in range(2):
            rows = slice(r * HALF, (r + 1) * HALF)
            chosen, rest = gathered[level][1][y, 0, r], gathered[level][1][y, 1, r]
            keep(ss.at[1], rows, x[rows, :BLK] - pick(bit, rest, chosen), slice(0, BLK))
            keep(ss.at[1], rows, x[rows, BLK:], slice(BLK, HALF))
        for rel in range(1, 4):
            from_sibling(level, 1, rel, 0)
        ext_copy(level).wait_recv()
        above = level + 1
        bit_y = bit_of(above, y)
        for kk in range(2):
            lower, upper, rows = merged(level, kk, 0)
            gathered[above][0][y, own_map(above), c, rows, :] = pick(bit_y, upper, lower)
            outer = pick(bit_y, lower, upper)
            if above == LEVELS - 1:
                gathered[above][1][y, own_map(above), c, rows, :] = outer
            else:
                raw[above, own_map(above), rows, :] = outer

    root_copy.wait()
    for level in reversed(range(LEVELS)):
        alpha, beta, alpha_out, beta_out, coupling = (mats.at[level, i] for i in range(5))
        upper_half = own_map(level)
        for k in range(8):
            rows = slice((k % 2 * 4 + k // 2) * BLK, (k % 2 * 4 + k // 2 + 1) * BLK)
            keep(fs, rows, p[k * BLK : (k + 1) * BLK, :])
        if level == LEVELS - 1:
            first, second = slice(0, IFACE), slice(IFACE, 2 * IFACE)
            x = mm(pair(alpha_out), (fs[0, first], fs[1, first]))
            t32[0] = x
            keep(ts, everything, x)
            x = mm(pair(beta), pair(ts)) - mm(pair(beta_out), (fs[0, second], fs[1, second]))
            keep(ds, everything, x)
            x = mm(pair(coupling), pair(ds))
            t32[1] = x
            keep(ts, everything, x)
            x = mm(pair(alpha), pair(ts))
            t32[0] = pick(upper_half, -(t32[0] + x), t32[1])
        else:
            t32[0] = mm(pair(down.at[level]), pair(fs))
        target = p if level else out.at[0]
        for k in range(4):
            bit = bit_of(level, k)
            near = t32[0, k * BLK : (k + 1) * BLK, :]
            f1 = p[2 * k * BLK : (2 * k + 1) * BLK, :]
            f2 = p[(2 * k + 1) * BLK : (2 * k + 2) * BLK, :]
            away = pick(upper_half, f2, f1)
            target[2 * k * BLK : (2 * k + 1) * BLK, :] = pick(bit, away, near)
            target[(2 * k + 1) * BLK : (2 * k + 2) * BLK, :] = pick(bit, near, away)

    for level in range(LEVELS):
        mine = own_map(level)
        for phase in range(2):
            whole = unit(level, phase, y, 0)
            parted = half(whole, 0)
            inner_top = level == LEVELS - 1 and not phase
            if level + phase:
                copy(level, phase, parted if inner_top else whole, ACROSS, left).wait_send()
            for index in range(SIBLING, BESIDE):
                copy(level, phase, whole, index, left).wait_send()
            if inner_top:
                for index in range(RIGHT, SIBLING):
                    copy(level, phase, parted, index, left).wait_send()
                for index in range(BESIDE + 2, COPIES):
                    copy(level, phase, parted, index, left).wait_send()
                copy(level, phase, parted, BESIDE + 1 - mine, left).wait_send()
            elif level == 1 and phase:
                sent(level, phase, 0, (RIGHT, LEFT, FAR))
                for rel in range(1, 4):
                    copy(level, phase, parted, BESIDE + 2 * rel + 1, left).wait_send()
                for index in (RIGHT, LEFT, FAR):
                    copy(level, phase, parted, index + 1, left).wait_send()
            elif level == 1:
                sent(level, 0, mine, (RIGHT, LEFT, FAR))
                sent(level, 0, 1 - mine, (FAR,))
            else:
                for u in range(2):
                    sent(level, phase, u, (RIGHT, LEFT, FAR))
    for level in range(2):
        ext_copy(level).wait_send()


def shards(leaf_maps, interface_blocks, root_data):
    vmem = pl.BlockSpec(memory_space=pltpu.VMEM)
    units = pltpu.VMEM((4, 2, 2, HALF, BLK), F32)
    return pl.pallas_call(
        kernel,
        out_shape=jax.ShapeDtypeStruct((1,) + root_data.shape[1:], F32),
        in_specs=[
            pl.BlockSpec(memory_space=pltpu.SMEM),
            vmem,
            pl.BlockSpec(memory_space=pl.ANY),
        ],
        out_specs=vmem,
        scratch_shapes=[units] * 6
        + [
            pltpu.VMEM((LEVELS, 2, HALF, BLK), F32),
            pltpu.VMEM((2, HALF, BLK), F32),
            pltpu.VMEM((2, 2, IFACE, 2 * IFACE), BF16),
            pltpu.VMEM((LEVELS, 5, 2, IFACE, IFACE), BF16),
            pltpu.VMEM((4, 2, IFACE, IFACE), BF16),
            pltpu.VMEM((2, IFACE, IFACE), F32),
            pltpu.VMEM((2, IFACE, HALF), BF16),
            pltpu.VMEM((IFACE, HALF), F32),
            pltpu.VMEM((2, 2, IFACE, HALF), BF16),
            pltpu.VMEM((2, 2, HALF, BLK), F32),
            pltpu.VMEM((2, HALF, BLK), F32),
            pltpu.VMEM((2 * IFACE, BLK), F32),
            pltpu.VMEM((2, 2 * IFACE, BLK), BF16),
            pltpu.VMEM((2, IFACE, BLK), F32),
            pltpu.VMEM((2, IFACE, BLK), BF16),
            pltpu.VMEM((2, IFACE, BLK), BF16),
            pltpu.SemaphoreType.DMA((LEVELS, 2, COPIES)),
            pltpu.SemaphoreType.DMA((LEVELS, 2, COPIES)),
            pltpu.SemaphoreType.DMA((2,)),
            pltpu.SemaphoreType.DMA((2,)),
            pltpu.SemaphoreType.DMA,
        ],
        compiler_params=pltpu.CompilerParams(
            collective_id=0, has_side_effects=True, vmem_limit_bytes=56 * 2**20
        ),
        name="merge_and_sweep",
    )(interface_blocks, leaf_maps, root_data)


def solution(mesh):
    return jax.shard_map(
        shards,
        mesh=mesh,
        in_specs=(P("box", None, "col"), P(), P(None, None, "col")),
        out_specs=P("box", None, "col"),
        check_vma=False,
    )
```

```python
import functools

import jax
import jax.numpy as jnp
from jax import lax
from jax.experimental import pallas as pl
from jax.experimental.pallas import tpu as pltpu
from jax.sharding import PartitionSpec as P

LEVELS = 3
IFACE = 512
BLK = 128
HALF = 256
F32 = jnp.float32
BF16 = jnp.bfloat16
MESH = pl.DeviceIdType.MESH

ACROSS, RIGHT, LEFT, FAR, SIBLING, BESIDE, COPIES = 0, 1, 3, 5, 7, 15, 23


def split(x):
    high = x.astype(BF16)
    return high, (x - high.astype(F32)).astype(BF16)


def mm(a, b):
    dot = functools.partial(jnp.dot, preferred_element_type=F32)
    return dot(a[0], b[0]) + (dot(a[0], b[1]) + dot(a[1], b[0]))


def mm_nt(a, b):
    dot = functools.partial(
        lax.dot_general, dimension_numbers=(((1,), (1,)), ((), ())), preferred_element_type=F32
    )
    return dot(a[0], b[0]) + (dot(a[0], b[1]) + dot(a[1], b[0]))


def pick(flag, yes, no):
    return jnp.where(jnp.broadcast_to(flag, yes.shape) == 1, yes, no)


def kernel(
    table, leaf, root, out,
    g0i, g0o, g1i, g1o, g2i, g2o,
    raw, both, down, mats, work, wf, vs, vf, ss, ext, dall, pr, p, fs, t32, ts, ds,
    send_sem, recv_sem, ext_send, ext_recv, root_sem,
):
    pos = lax.axis_index("box")
    y = lax.axis_index("col")
    c = pos % 2
    gathered = ((g0i, g0o), (g1i, g1o), (g2i, g2o))
    slots = (y, (y + 3) % 4, (y + 1) % 4, (y + 2) % 4)
    right, left, opposite, sibling = (pos, slots[2]), (pos, slots[1]), (pos, slots[3]), (pos ^ 1, y)

    root_copy = pltpu.make_async_copy(root.at[pos // 8], pr, root_sem)
    root_copy.start()

    barrier = pltpu.get_barrier_semaphore()
    for peer in (right, left, opposite, sibling, (pos ^ 2, y), (pos ^ 4, y)):
        pl.semaphore_signal(barrier, inc=1, device_id=peer, device_id_type=MESH)

    def own_map(level):
        return (pos >> level) & 1

    def bit_of(level, k):
        return table[level, pos - pos % 2**level, k] & 1

    def next_bit(level, k):
        return bit_of(level + 1, k) if level + 1 < LEVELS else jnp.int32(0)

    def unit(level, phase, slot, u):
        g = gathered[level][phase]
        return g.at[slot, c, u] if level + phase == 0 else g.at[slot, u, c]

    def copy(level, phase, ref, index, peer, src=None):
        return pltpu.make_async_remote_copy(
            src_ref=ref if src is None else src,
            dst_ref=ref,
            send_sem=send_sem.at[level, phase, index],
            recv_sem=recv_sem.at[level, phase, index],
            device_id=peer,
            device_id_type=MESH,
        )

    def send(*args):
        copy(*args).start()

    z_low = (pos >> 1) & 1
    beside = (pos ^ 2, y)

    def half(ref, which):
        return ref.at[which]

    def to_beside(level, phase, rel, u):
        ref = half(unit(level, phase, slots[rel], u), z_low)
        send(level, phase, ref, BESIDE + 2 * rel + u, beside)

    def split_around(level, phase, u):
        ref = half(unit(level, phase, y, u), z_low)
        send(level, phase, ref, RIGHT + u, right)
        send(level, phase, ref, LEFT + u, left)
        send(level, phase, ref, FAR + u, opposite)

    def serve_split(level, phase, u):
        for rel in (1, 2, 3):
            ref = half(unit(level, phase, slots[rel], u), z_low)
            copy(level, phase, ref, (0, RIGHT, LEFT, FAR)[rel] + u, left).wait_recv()
            to_beside(level, phase, rel, u)

    def join_split(level, phase, u, rels=(1, 2, 3)):
        for rel in rels:
            ref = half(unit(level, phase, slots[rel], u), 1 - z_low)
            copy(level, phase, ref, BESIDE + 2 * rel + u, beside).wait_recv()
            to_sibling(level, phase, rel, u)

    def to_sibling(level, phase, rel, u):
        send(level, phase, unit(level, phase, slots[rel], u), SIBLING + 2 * rel + u, sibling)

    def from_sibling(level, phase, rel, u):
        ref = unit(level, phase, slots[rel], u)
        copy(level, phase, ref, SIBLING + 2 * rel + u, sibling).wait_recv()

    def send_next(level, phase, u):
        ref = unit(level, phase, y, u)
        send(level, phase, ref, RIGHT + u, right)
        send(level, phase, ref, LEFT + u, left)

    def send_far(level, phase, u):
        send(level, phase, unit(level, phase, y, u), FAR + u, opposite)

    def send_around(level, phase, u):
        send_next(level, phase, u)
        send_far(level, phase, u)

    def sent(level, phase, u, kinds):
        ref = unit(level, phase, y, u)
        for index in kinds:
            copy(level, phase, ref, index + u, right).wait_send()

    def arrived(level, phase, rel, u):
        index = (0, RIGHT, LEFT, FAR)[rel] + u
        copy(level, phase, unit(level, phase, slots[rel], u), index, left).wait_recv()

    def relay_far(level):
        mine = own_map(level)
        ref = unit(level, 0, slots[3], mine)
        pltpu.make_async_remote_copy(
            src_ref=ref,
            dst_ref=ref,
            send_sem=send_sem.at[level, 0, FAR + 1 - mine],
            recv_sem=recv_sem.at[level, 0, FAR + mine],
            device_id=(pos ^ 2**level, y),
            device_id_type=MESH,
        ).start()

    def serve(level, phase, u, rels=(1, 2, 3)):
        for rel in rels:
            arrived(level, phase, rel, u)
            to_sibling(level, phase, rel, u)

    def rows_of(rel):
        return pl.ds(pl.multiple_of(slots[rel] * BLK, BLK), BLK)

    def block(k):
        return slice(k * BLK, (k + 1) * BLK)

    def keep(ref, rows, x, columns=slice(None)):
        high, low = split(x)
        ref[0, rows, columns] = high
        ref[1, rows, columns] = low

    def keep_inner(level, rel, m):
        for k in range(4):
            x = gathered[level][0][slots[rel], m, k // 2, k % 2]
            keep(mats.at[level, m], rows_of(rel), x, block(k))

    def keep_outer(level, rel, awaited=(0, 1)):
        for q in awaited:
            from_sibling(level, 1, rel, q)
        bit = next_bit(level, slots[rel])
        g = gathered[level][1]
        for k in range(4):
            chosen, rest = g[slots[rel], 0, k // 2, k % 2], g[slots[rel], 1, k // 2, k % 2]
            keep(mats.at[level, 2], rows_of(rel), pick(bit, rest, chosen), block(k))
            keep(mats.at[level, 3], rows_of(rel), pick(bit, chosen, rest), block(k))

    def pair(ref):
        return ref[0], ref[1]

    everything = slice(None)

    def order_outer(level):
        theirs = 1 - own_map(level)
        copy(level, 1, raw.at[level, theirs], ACROSS, sibling).wait_recv()
        bit = next_bit(level, y)
        g = gathered[level][1]
        g[y, 0, c] = pick(bit, raw[level, 1], raw[level, 0])
        g[y, 1, c] = pick(bit, raw[level, 0], raw[level, 1])
        to_sibling(level, 1, 0, 0)
        to_sibling(level, 1, 0, 1)

    def finish_cubes(level):
        one, two, four, three = (work.at[i] for i in range(4))
        x = mm(pair(one), pair(two)) + wf[0] + wf[1]
        row = lax.broadcasted_iota(jnp.int32, x.shape, 0)
        column = lax.broadcasted_iota(jnp.int32, x.shape, 1)
        x = x + jnp.where(row == column, 1.0, 0.0)
        wf[0] = x
        keep(three, everything, x)
        keep(four, everything, mm(pair(two), pair(two)))

    def finish_coupling(level):
        keep(mats.at[level, 4], everything, wf[0] + mm(pair(work.at[3]), pair(work.at[2])))

    def sweep_operator(level):
        alpha, beta, alpha_out, beta_out, coupling = (mats.at[level, i] for i in range(5))
        x = mm(pair(alpha_out), pair(beta))
        keep(work.at[0], everything, x)
        keep(down.at[level], slice(0, IFACE), mm(pair(work.at[0]), pair(coupling)))
        keep(down.at[level], slice(IFACE, 2 * IFACE), -mm(pair(beta_out), pair(coupling)))

    def sweep_operator_beta(level):
        upper_half = own_map(level)
        for i in range(2):
            rows = slice(i * IFACE, (i + 1) * IFACE)
            near = (down[level, 0, rows, :], down[level, 1, rows, :])
            x = -mm(near, pair(mats.at[level, 0]))
            if i == 0:
                x = x - (mats[level, 2, 0].astype(F32) + mats[level, 2, 1].astype(F32))
            held = near[0].astype(F32) + near[1].astype(F32)
            keep(down.at[level], rows, pick(upper_half, x, held))

    def ext_copy(level):
        return pltpu.make_async_remote_copy(
            src_ref=dall.at[1 - c] if level == 0 else ext.at[1, own_map(1)],
            dst_ref=ext.at[level, own_map(level)],
            send_sem=ext_send.at[level],
            recv_sem=ext_recv.at[level],
            device_id=(pos ^ 2**level, y),
            device_id_type=MESH,
        )

    def merged(level, kk, rest):
        k = 2 * c + kk
        bit = bit_of(level + 1, k)
        part = 1 - bit if rest else bit
        g = gathered[level][1]
        r = split(jnp.concatenate([g[k, rest, i // 2, i % 2] for i in range(4)], 1))
        x = mm_nt((ss[part, 0], ss[part, 1]), r)
        kept = pick(part, ext[level, 1, kk], ext[level, 0, kk])
        lower = x[:BLK] + pick(part, jnp.zeros_like(kept), kept)
        upper = x[BLK:] + pick(part, kept, jnp.zeros_like(kept))
        return lower, upper

    bit_y = bit_of(0, y)
    for k in range(4):
        bit = bit_of(0, k)
        even = leaf[0, 2 * k * BLK : (2 * k + 1) * BLK, :]
        odd = leaf[0, (2 * k + 1) * BLK : (2 * k + 2) * BLK, :]
        near = pick(bit, odd, even).T
        away = pick(bit, even, odd).T
        g0i[y, c, k // 2, k % 2] = pick(bit_y, near[BLK:], near[:BLK])
        both[k // 2, k % 2] = pick(bit_y, near[:BLK], near[BLK:])
        dall[k // 2, k % 2] = pick(bit_y, away[:BLK], away[BLK:])

    pl.semaphore_wait(barrier, 6)

    for level in range(LEVELS):
        alpha, beta, alpha_out, beta_out, coupling = (mats.at[level, i] for i in range(5))
        one, two, four, three = (work.at[i] for i in range(4))
        mine = own_map(level)
        if level == 0:
            first, second = unit(0, 0, y, 0), unit(0, 0, y, 1)
            send(0, 0, first, RIGHT, right)
            send(0, 0, second, LEFT + 1, left)
            send(0, 0, second, RIGHT + 1, right)
            send(0, 0, first, LEFT, left)
            to_sibling(0, 0, 0, 0)
            to_sibling(0, 0, 0, 1)
            send(0, 1, raw.at[0, mine], ACROSS, sibling, both.at[1 - c])
            ext_copy(0).start()
            raw[0, mine] = both[c]
            ext[0, mine] = dall[c]
            order_outer(0)
            for u in range(2):
                from_sibling(0, 0, 0, u)
            keep_inner(0, 0, 0)
            keep_inner(0, 0, 1)
            arrived(0, 0, 1, 0)
            send(0, 0, unit(0, 0, slots[1], 0), FAR, right)
            to_sibling(0, 0, 1, 0)
            arrived(0, 0, 2, 1)
            send(0, 0, unit(0, 0, slots[2], 1), FAR + 1, left)
            to_sibling(0, 0, 2, 1)
            keep_outer(0, 0)
            arrived(0, 0, 1, 1)
            to_sibling(0, 0, 1, 1)
            arrived(0, 0, 2, 0)
            to_sibling(0, 0, 2, 0)
            send_around(0, 1, 0)
            for rel in (1, 2):
                for u in range(2):
                    from_sibling(0, 0, rel, u)
                keep_inner(0, rel, 0)
                keep_inner(0, rel, 1)
            for u in range(2):
                arrived(0, 0, 3, u)
                to_sibling(0, 0, 3, u)
            for u in range(2):
                from_sibling(0, 0, 3, u)
            keep_inner(0, 3, 0)
            keep_inner(0, 3, 1)
        else:
            theirs = 1 - mine
            last = level == LEVELS - 1
            partner = (pos ^ 2**level, y)
            if last:
                send(level, 0, half(unit(level, 0, y, mine), z_low), ACROSS, partner)
                split_around(level, 0, mine)
                to_sibling(level, 0, 0, mine)
                send(level, 1, unit(level, 1, y, mine), ACROSS, partner)
                to_sibling(level, 1, 0, mine)
                finish_cubes(level - 1)
                serve_split(level - 1, 1, 1)
                finish_coupling(level - 1)
                send_next(level, 1, mine)
                ref = half(unit(level, 0, y, theirs), z_low)
                copy(level, 0, ref, ACROSS, partner).wait_recv()
                split_around(level, 0, theirs)
                to_beside(level, 0, 0, theirs)
                serve_split(level, 0, mine)
                join_split(level - 1, 1, 1)
                join_split(level, 0, theirs, (0,))
                for rel in range(1, 4):
                    keep_outer(level - 1, rel, (1,))
                send_far(level, 1, mine)
                join_split(level, 0, mine)
                sweep_operator(1)
                serve_split(level, 0, theirs)
                copy(level, 1, unit(level, 1, y, theirs), ACROSS, partner).wait_recv()
                to_sibling(level, 1, 0, theirs)
                send_around(level, 1, theirs)
                for rel in range(4):
                    from_sibling(level, 0, rel, mine)
                    keep_inner(level, rel, mine)
                keep_outer(level, 0)
                sweep_operator_beta(1)
                join_split(level, 0, theirs)
                for rel in range(4):
                    from_sibling(level, 0, rel, theirs)
                    keep_inner(level, rel, theirs)
            else:
                send(level, 0, unit(level, 0, y, mine), ACROSS, partner)
                send_around(level, 0, mine)
                to_sibling(level, 0, 0, mine)
                send(level, 1, raw.at[level, mine], ACROSS, partner)
                finish_cubes(level - 1)
                copy(level, 0, unit(level, 0, y, theirs), ACROSS, partner).wait_recv()
                send_next(level, 0, theirs)
                to_sibling(level, 0, 0, theirs)
                order_outer(level)
                serve(level - 1, 1, 1)
                serve(level, 0, mine)
                relay_far(level)
                finish_coupling(level - 1)
                for rel in range(1, 4):
                    keep_outer(level - 1, rel, (1,))
                bit_y = bit_of(1, y)
                for kk in range(2):
                    lower, upper = merged(0, kk, 1)
                    ext[1, mine, kk] = pick(bit_y, lower, upper)
                ext_copy(1).start()
                sent(level, 0, theirs, (RIGHT, LEFT))
                send_around(level, 1, 0)
                sweep_operator(0)
                root_copy.wait()
                for k in range(8):
                    p[k] = pr[block(k), :].T
                for rel in range(4):
                    from_sibling(level, 0, rel, mine)
                    keep_inner(level, rel, mine)
                keep_outer(level, 0)
                serve(level, 0, theirs, (1, 2))
                sweep_operator_beta(0)
                for rel in range(3):
                    from_sibling(level, 0, rel, theirs)
                    keep_inner(level, rel, theirs)
                serve(level, 0, theirs, (3,))
                from_sibling(level, 0, 3, theirs)
                keep_inner(level, 3, theirs)

        if level == LEVELS - 1:
            x = mm(pair(alpha), pair(beta))
            wf[0] = x
            keep(one, everything, x)
            serve(level, 1, mine)
            x = mm(pair(one), pair(one))
            wf[1] = x
            keep(two, everything, x)
            finish_cubes(level)
            finish_coupling(level)
            serve(level, 1, theirs)
            for rel in range(1, 4):
                keep_outer(level, rel)
            break

        own = rows_of(0)
        bit = next_bit(level, y)
        g = gathered[level][1]
        x = mm(
            [jnp.concatenate([alpha[i], alpha_out[i, own, :]], 0) for i in range(2)],
            pair(beta),
        )
        wf[0] = x[:IFACE]
        keep(one, everything, x[:IFACE])
        vf[:BLK, :] = x[IFACE:]
        for k in range(4):
            chosen, rest = g[y, 0, k // 2, k % 2], g[y, 1, k // 2, k % 2]
            vf[BLK:, block(k)] = -pick(bit, chosen, rest)
        keep(vs, everything, vf[...])
        x = mm([jnp.concatenate([one[i], vs[i]], 0) for i in range(2)], pair(one))
        wf[1] = x[:IFACE]
        keep(two, everything, x[:IFACE])
        x = vf[...] + x[IFACE:]
        vf[...] = x
        keep(vs, everything, x)
        (send_around if level == 0 else split_around)(level, 1, 1)
        x = vf[...] + mm(pair(vs), pair(two))
        vf[...] = x
        keep(vs, everything, x)
        keep(vs, everything, mm(pair(vs), pair(two)))
        serve(level, 1, 0)
        x = vf[...] + mm(pair(vs), pair(two))
        keep(ss.at[0], everything, x)
        x = -mm(pair(ss.at[0]), pair(alpha))
        keep(ss.at[1], slice(BLK, HALF), x[BLK:])
        for k in range(4):
            chosen, rest = g[y, 0, k // 2, k % 2], g[y, 1, k // 2, k % 2]
            keep(ss.at[1], slice(0, BLK), x[:BLK, block(k)] - pick(bit, rest, chosen), block(k))
        for rel in range(1, 4):
            from_sibling(level, 1, rel, 0)
        ext_copy(level).wait_recv()
        above = level + 1
        bit_y = bit_of(above, y)
        for kk in range(2):
            lower, upper = merged(level, kk, 0)
            gathered[above][0][y, own_map(above), c, kk] = pick(bit_y, upper, lower)
            outer = pick(bit_y, lower, upper)
            if above == LEVELS - 1:
                gathered[above][1][y, own_map(above), c, kk] = outer
            else:
                raw[above, own_map(above), kk] = outer

    for level in reversed(range(LEVELS)):
        alpha, beta, alpha_out, beta_out, coupling = (mats.at[level, i] for i in range(5))
        upper_half = own_map(level)
        for k in range(8):
            keep(fs, everything, p[k], block(k % 2 * 4 + k // 2))
        if level == LEVELS - 1:
            first, second = slice(0, IFACE), slice(IFACE, 2 * IFACE)
            x = mm((fs[0, :, first], fs[1, :, first]), pair(alpha_out))
            t32[0] = x
            keep(ts, everything, x)
            x = mm(pair(ts), pair(beta)) - mm((fs[0, :, second], fs[1, :, second]), pair(beta_out))
            keep(ds, everything, x)
            x = mm(pair(ds), pair(coupling))
            t32[1] = x
            keep(ts, everything, x)
            x = mm(pair(ts), pair(alpha))
            t32[0] = pick(upper_half, -(t32[0] + x), t32[1])
        else:
            t32[0] = mm(pair(fs), pair(down.at[level]))
        for k in range(4):
            bit = bit_of(level, k)
            near = t32[0, :, block(k)]
            away = pick(upper_half, p[2 * k + 1], p[2 * k])
            even, odd = pick(bit, away, near), pick(bit, near, away)
            if level:
                p[2 * k] = even
                p[2 * k + 1] = odd
            else:
                out[0, block(2 * k), :] = even.T
                out[0, block(2 * k + 1), :] = odd.T

    for level in range(LEVELS):
        mine = own_map(level)
        for phase in range(2):
            whole = unit(level, phase, y, 0)
            parted = half(whole, 0)
            inner_top = level == LEVELS - 1 and not phase
            if level + phase:
                copy(level, phase, parted if inner_top else whole, ACROSS, left).wait_send()
            for index in range(SIBLING, BESIDE):
                copy(level, phase, whole, index, left).wait_send()
            if inner_top:
                for index in range(RIGHT, SIBLING):
                    copy(level, phase, parted, index, left).wait_send()
                for index in range(BESIDE + 2, COPIES):
                    copy(level, phase, parted, index, left).wait_send()
                copy(level, phase, parted, BESIDE + 1 - mine, left).wait_send()
            elif level == 1 and phase:
                sent(level, phase, 0, (RIGHT, LEFT, FAR))
                for rel in range(1, 4):
                    copy(level, phase, parted, BESIDE + 2 * rel + 1, left).wait_send()
                for index in (RIGHT, LEFT, FAR):
                    copy(level, phase, parted, index + 1, left).wait_send()
            elif level == 1:
                sent(level, 0, mine, (RIGHT, LEFT, FAR))
                sent(level, 0, 1 - mine, (FAR,))
            else:
                for u in range(2):
                    sent(level, phase, u, (RIGHT, LEFT, FAR))
    for level in range(2):
        ext_copy(level).wait_send()


def shards(leaf_maps, interface_blocks, root_data):
    vmem = pl.BlockSpec(memory_space=pltpu.VMEM)
    units = pltpu.VMEM((4, 2, 2, 2, BLK, BLK), F32)
    return pl.pallas_call(
        kernel,
        out_shape=jax.ShapeDtypeStruct((1,) + root_data.shape[1:], F32),
        in_specs=[
            pl.BlockSpec(memory_space=pltpu.SMEM),
            vmem,
            pl.BlockSpec(memory_space=pl.ANY),
        ],
        out_specs=vmem,
        scratch_shapes=[units] * 6
        + [
            pltpu.VMEM((LEVELS, 2, 2, BLK, BLK), F32),
            pltpu.VMEM((2, 2, BLK, BLK), F32),
            pltpu.VMEM((2, 2, 2 * IFACE, IFACE), BF16),
            pltpu.VMEM((LEVELS, 5, 2, IFACE, IFACE), BF16),
            pltpu.VMEM((4, 2, IFACE, IFACE), BF16),
            pltpu.VMEM((2, IFACE, IFACE), F32),
            pltpu.VMEM((2, HALF, IFACE), BF16),
            pltpu.VMEM((HALF, IFACE), F32),
            pltpu.VMEM((2, 2, HALF, IFACE), BF16),
            pltpu.VMEM((2, 2, 2, BLK, BLK), F32),
            pltpu.VMEM((2, 2, BLK, BLK), F32),
            pltpu.VMEM((2 * IFACE, BLK), F32),
            pltpu.VMEM((8, BLK, BLK), F32),
            pltpu.VMEM((2, BLK, 2 * IFACE), BF16),
            pltpu.VMEM((2, BLK, IFACE), F32),
            pltpu.VMEM((2, BLK, IFACE), BF16),
            pltpu.VMEM((2, BLK, IFACE), BF16),
            pltpu.SemaphoreType.DMA((LEVELS, 2, COPIES)),
            pltpu.SemaphoreType.DMA((LEVELS, 2, COPIES)),
            pltpu.SemaphoreType.DMA((2,)),
            pltpu.SemaphoreType.DMA((2,)),
            pltpu.SemaphoreType.DMA,
        ],
        compiler_params=pltpu.CompilerParams(
            collective_id=0, has_side_effects=True, vmem_limit_bytes=56 * 2**20
        ),
        name="merge_and_sweep",
    )(interface_blocks, leaf_maps, root_data)


def solution(mesh):
    return jax.shard_map(
        shards,
        mesh=mesh,
        in_specs=(P("box", None, "col"), P(), P(None, None, "col")),
        out_specs=P("box", None, "col"),
        check_vma=False,
    )
```

```python
import functools

import jax
import jax.numpy as jnp
from jax import lax
from jax.experimental import pallas as pl
from jax.experimental.pallas import tpu as pltpu
from jax.sharding import PartitionSpec as P

LEVELS = 3
IFACE = 512
BLK = 128
HALF = 256
F32 = jnp.float32
BF16 = jnp.bfloat16
MESH = pl.DeviceIdType.MESH

ACROSS, RIGHT, LEFT, FAR, SIBLING, BESIDE, COPIES = 0, 1, 3, 5, 7, 15, 23


def split(x):
    high = x.astype(BF16)
    return high, (x - high.astype(F32)).astype(BF16)


def mm(a, b):
    dot = functools.partial(jnp.dot, preferred_element_type=F32)
    return dot(a[0], b[0]) + (dot(a[0], b[1]) + dot(a[1], b[0]))


def mm_nt(a, b):
    dot = functools.partial(
        lax.dot_general, dimension_numbers=(((1,), (1,)), ((), ())), preferred_element_type=F32
    )
    return dot(a[0], b[0]) + (dot(a[0], b[1]) + dot(a[1], b[0]))


def pick(flag, yes, no):
    return jnp.where(jnp.broadcast_to(flag, yes.shape) == 1, yes, no)


def kernel(
    table, leaf, root, out,
    g0i, g0o, g1i, g1o, g2i, g2o,
    raw, both, down, mats, work, wf, vs, vf, ss, ext, dall, pr, p, fs, t32, ts, ds,
    send_sem, recv_sem, ext_send, ext_recv, root_sem,
):
    pos = lax.axis_index("box")
    y = lax.axis_index("col")
    c = pos % 2
    gathered = ((g0i, g0o), (g1i, g1o), (g2i, g2o))
    slots = (y, (y + 3) % 4, (y + 1) % 4, (y + 2) % 4)
    right, left, opposite, sibling = (pos, slots[2]), (pos, slots[1]), (pos, slots[3]), (pos ^ 1, y)

    root_copy = pltpu.make_async_copy(root.at[pos // 8], pr, root_sem)
    root_copy.start()

    barrier = pltpu.get_barrier_semaphore()
    for peer in (right, left, opposite, sibling, (pos ^ 2, y), (pos ^ 4, y)):
        pl.semaphore_signal(barrier, inc=1, device_id=peer, device_id_type=MESH)

    def own_map(level):
        return (pos >> level) & 1

    def bit_of(level, k):
        return table[level, k, pos - pos % 2**level] & 1

    def next_bit(level, k):
        return bit_of(level + 1, k) if level + 1 < LEVELS else jnp.int32(0)

    def unit(level, phase, slot, u):
        g = gathered[level][phase]
        return g.at[slot, c, u] if level + phase == 0 else g.at[slot, u, c]

    def copy(level, phase, ref, index, peer, src=None):
        return pltpu.make_async_remote_copy(
            src_ref=ref if src is None else src,
            dst_ref=ref,
            send_sem=send_sem.at[level, phase, index],
            recv_sem=recv_sem.at[level, phase, index],
            device_id=peer,
            device_id_type=MESH,
        )

    def send(*args):
        copy(*args).start()

    z_low = (pos >> 1) & 1
    beside = (pos ^ 2, y)

    def half(ref, which):
        return ref.at[which]

    def to_beside(level, phase, rel, u):
        ref = half(unit(level, phase, slots[rel], u), z_low)
        send(level, phase, ref, BESIDE + 2 * rel + u, beside)

    def split_around(level, phase, u):
        ref = half(unit(level, phase, y, u), z_low)
        send(level, phase, ref, RIGHT + u, right)
        send(level, phase, ref, LEFT + u, left)
        send(level, phase, ref, FAR + u, opposite)

    def serve_split(level, phase, u):
        for rel in (1, 2, 3):
            ref = half(unit(level, phase, slots[rel], u), z_low)
            copy(level, phase, ref, (0, RIGHT, LEFT, FAR)[rel] + u, left).wait_recv()
            to_beside(level, phase, rel, u)

    def join_split(level, phase, u, rels=(1, 2, 3)):
        for rel in rels:
            ref = half(unit(level, phase, slots[rel], u), 1 - z_low)
            copy(level, phase, ref, BESIDE + 2 * rel + u, beside).wait_recv()
            to_sibling(level, phase, rel, u)

    def to_sibling(level, phase, rel, u):
        send(level, phase, unit(level, phase, slots[rel], u), SIBLING + 2 * rel + u, sibling)

    def from_sibling(level, phase, rel, u):
        ref = unit(level, phase, slots[rel], u)
        copy(level, phase, ref, SIBLING + 2 * rel + u, sibling).wait_recv()

    def send_next(level, phase, u):
        ref = unit(level, phase, y, u)
        send(level, phase, ref, RIGHT + u, right)
        send(level, phase, ref, LEFT + u, left)

    def send_far(level, phase, u):
        send(level, phase, unit(level, phase, y, u), FAR + u, opposite)

    def send_around(level, phase, u):
        send_next(level, phase, u)
        send_far(level, phase, u)

    def sent(level, phase, u, kinds):
        ref = unit(level, phase, y, u)
        for index in kinds:
            copy(level, phase, ref, index + u, right).wait_send()

    def arrived(level, phase, rel, u):
        index = (0, RIGHT, LEFT, FAR)[rel] + u
        copy(level, phase, unit(level, phase, slots[rel], u), index, left).wait_recv()

    def relay_far(level):
        mine = own_map(level)
        ref = unit(level, 0, slots[3], mine)
        pltpu.make_async_remote_copy(
            src_ref=ref,
            dst_ref=ref,
            send_sem=send_sem.at[level, 0, FAR + 1 - mine],
            recv_sem=recv_sem.at[level, 0, FAR + mine],
            device_id=(pos ^ 2**level, y),
            device_id_type=MESH,
        ).start()

    def serve(level, phase, u, rels=(1, 2, 3)):
        for rel in rels:
            arrived(level, phase, rel, u)
            to_sibling(level, phase, rel, u)

    def rows_of(rel):
        return pl.ds(pl.multiple_of(slots[rel] * BLK, BLK), BLK)

    def block(k):
        return slice(k * BLK, (k + 1) * BLK)

    def keep(ref, rows, x, columns=slice(None)):
        high, low = split(x)
        ref[0, rows, columns] = high
        ref[1, rows, columns] = low

    def keep_inner(level, rel, m):
        for k in range(4):
            x = gathered[level][0][slots[rel], m, k // 2, k % 2]
            keep(mats.at[level, m], rows_of(rel), x, block(k))

    def keep_outer(level, rel, awaited=(0, 1)):
        for q in awaited:
            from_sibling(level, 1, rel, q)
        bit = next_bit(level, slots[rel])
        g = gathered[level][1]
        for k in range(4):
            chosen, rest = g[slots[rel], 0, k // 2, k % 2], g[slots[rel], 1, k // 2, k % 2]
            keep(mats.at[level, 2], rows_of(rel), pick(bit, rest, chosen), block(k))
            keep(mats.at[level, 3], rows_of(rel), pick(bit, chosen, rest), block(k))

    def pair(ref):
        return ref[0], ref[1]

    everything = slice(None)

    def order_outer(level):
        theirs = 1 - own_map(level)
        copy(level, 1, raw.at[level, theirs], ACROSS, sibling).wait_recv()
        bit = next_bit(level, y)
        g = gathered[level][1]
        g[y, 0, c] = pick(bit, raw[level, 1], raw[level, 0])
        g[y, 1, c] = pick(bit, raw[level, 0], raw[level, 1])
        to_sibling(level, 1, 0, 0)
        to_sibling(level, 1, 0, 1)

    def finish_cubes(level):
        one, two, four, three = (work.at[i] for i in range(4))
        x = mm(pair(one), pair(two)) + wf[0] + wf[1]
        row = lax.broadcasted_iota(jnp.int32, x.shape, 0)
        column = lax.broadcasted_iota(jnp.int32, x.shape, 1)
        x = x + jnp.where(row == column, 1.0, 0.0)
        wf[0] = x
        keep(three, everything, x)
        keep(four, everything, mm(pair(two), pair(two)))

    def finish_coupling(level):
        keep(mats.at[level, 4], everything, wf[0] + mm(pair(work.at[3]), pair(work.at[2])))

    def sweep_operator(level):
        alpha, beta, alpha_out, beta_out, coupling = (mats.at[level, i] for i in range(5))
        x = mm(pair(alpha_out), pair(beta))
        keep(work.at[0], everything, x)
        keep(down.at[level], slice(0, IFACE), mm(pair(work.at[0]), pair(coupling)))
        keep(down.at[level], slice(IFACE, 2 * IFACE), -mm(pair(beta_out), pair(coupling)))

    def sweep_operator_beta(level):
        upper_half = own_map(level)
        for i in range(2):
            rows = slice(i * IFACE, (i + 1) * IFACE)
            near = (down[level, 0, rows, :], down[level, 1, rows, :])
            x = -mm(near, pair(mats.at[level, 0]))
            if i == 0:
                x = x - (mats[level, 2, 0].astype(F32) + mats[level, 2, 1].astype(F32))
            held = near[0].astype(F32) + near[1].astype(F32)
            keep(down.at[level], rows, pick(upper_half, x, held))

    def ext_copy(level):
        return pltpu.make_async_remote_copy(
            src_ref=dall.at[1 - c] if level == 0 else ext.at[1, own_map(1)],
            dst_ref=ext.at[level, own_map(level)],
            send_sem=ext_send.at[level],
            recv_sem=ext_recv.at[level],
            device_id=(pos ^ 2**level, y),
            device_id_type=MESH,
        )

    def merged(level, kk, rest):
        k = 2 * c + kk
        bit = bit_of(level + 1, k)
        part = 1 - bit if rest else bit
        g = gathered[level][1]
        r = split(jnp.concatenate([g[k, rest, i // 2, i % 2] for i in range(4)], 1))
        x = mm_nt((ss[part, 0], ss[part, 1]), r)
        kept = pick(part, ext[level, 1, kk], ext[level, 0, kk])
        lower = x[:BLK] + pick(part, jnp.zeros_like(kept), kept)
        upper = x[BLK:] + pick(part, kept, jnp.zeros_like(kept))
        return lower, upper

    bit_y = bit_of(0, y)
    for k in range(4):
        bit = bit_of(0, k)
        even = leaf[0, 2 * k * BLK : (2 * k + 1) * BLK, :]
        odd = leaf[0, (2 * k + 1) * BLK : (2 * k + 2) * BLK, :]
        near = pick(bit, odd, even).T
        away = pick(bit, even, odd).T
        g0i[y, c, k // 2, k % 2] = pick(bit_y, near[BLK:], near[:BLK])
        both[k // 2, k % 2] = pick(bit_y, near[:BLK], near[BLK:])
        dall[k // 2, k % 2] = pick(bit_y, away[:BLK], away[BLK:])

    pl.semaphore_wait(barrier, 6)

    for level in range(LEVELS):
        alpha, beta, alpha_out, beta_out, coupling = (mats.at[level, i] for i in range(5))
        one, two, four, three = (work.at[i] for i in range(4))
        mine = own_map(level)
        if level == 0:
            first, second = unit(0, 0, y, 0), unit(0, 0, y, 1)
            send(0, 0, first, RIGHT, right)
            send(0, 0, second, LEFT + 1, left)
            send(0, 0, second, RIGHT + 1, right)
            send(0, 0, first, LEFT, left)
            to_sibling(0, 0, 0, 0)
            to_sibling(0, 0, 0, 1)
            send(0, 1, raw.at[0, mine], ACROSS, sibling, both.at[1 - c])
            ext_copy(0).start()
            raw[0, mine] = both[c]
            ext[0, mine] = dall[c]
            order_outer(0)
            for u in range(2):
                from_sibling(0, 0, 0, u)
            keep_inner(0, 0, 0)
            keep_inner(0, 0, 1)
            arrived(0, 0, 1, 0)
            send(0, 0, unit(0, 0, slots[1], 0), FAR, right)
            to_sibling(0, 0, 1, 0)
            arrived(0, 0, 2, 1)
            send(0, 0, unit(0, 0, slots[2], 1), FAR + 1, left)
            to_sibling(0, 0, 2, 1)
            keep_outer(0, 0)
            arrived(0, 0, 1, 1)
            to_sibling(0, 0, 1, 1)
            arrived(0, 0, 2, 0)
            to_sibling(0, 0, 2, 0)
            send_around(0, 1, 0)
            for rel in (1, 2):
                for u in range(2):
                    from_sibling(0, 0, rel, u)
                keep_inner(0, rel, 0)
                keep_inner(0, rel, 1)
            for u in range(2):
                arrived(0, 0, 3, u)
                to_sibling(0, 0, 3, u)
            for u in range(2):
                from_sibling(0, 0, 3, u)
            keep_inner(0, 3, 0)
            keep_inner(0, 3, 1)
        else:
            theirs = 1 - mine
            last = level == LEVELS - 1
            partner = (pos ^ 2**level, y)
            if last:
                send(level, 0, half(unit(level, 0, y, mine), z_low), ACROSS, partner)
                split_around(level, 0, mine)
                to_sibling(level, 0, 0, mine)
                send(level, 1, unit(level, 1, y, mine), ACROSS, partner)
                to_sibling(level, 1, 0, mine)
                finish_cubes(level - 1)
                serve_split(level - 1, 1, 1)
                send_next(level, 1, mine)
                sweep_operator_beta(0)
                finish_coupling(level - 1)
                ref = half(unit(level, 0, y, theirs), z_low)
                copy(level, 0, ref, ACROSS, partner).wait_recv()
                split_around(level, 0, theirs)
                to_beside(level, 0, 0, theirs)
                serve_split(level, 0, mine)
                join_split(level - 1, 1, 1)
                join_split(level, 0, theirs, (0,))
                for rel in range(1, 4):
                    keep_outer(level - 1, rel, (1,))
                send_far(level, 1, mine)
                join_split(level, 0, mine)
                serve_split(level, 0, theirs)
                copy(level, 1, unit(level, 1, y, theirs), ACROSS, partner).wait_recv()
                to_sibling(level, 1, 0, theirs)
                send_around(level, 1, theirs)
                sweep_operator(1)
                for rel in range(4):
                    from_sibling(level, 0, rel, mine)
                    keep_inner(level, rel, mine)
                keep_outer(level, 0)
                sweep_operator_beta(1)
                join_split(level, 0, theirs)
                for rel in range(4):
                    from_sibling(level, 0, rel, theirs)
                    keep_inner(level, rel, theirs)
            else:
                send(level, 0, unit(level, 0, y, mine), ACROSS, partner)
                send_around(level, 0, mine)
                to_sibling(level, 0, 0, mine)
                send(level, 1, raw.at[level, mine], ACROSS, partner)
                finish_cubes(level - 1)
                copy(level, 0, unit(level, 0, y, theirs), ACROSS, partner).wait_recv()
                send_next(level, 0, theirs)
                to_sibling(level, 0, 0, theirs)
                order_outer(level)
                serve(level - 1, 1, 1)
                serve(level, 0, mine)
                relay_far(level)
                finish_coupling(level - 1)
                for rel in range(1, 4):
                    keep_outer(level - 1, rel, (1,))
                bit_y = bit_of(1, y)
                for kk in range(2):
                    lower, upper = merged(0, kk, 1)
                    ext[1, mine, kk] = pick(bit_y, lower, upper)
                ext_copy(1).start()
                sent(level, 0, theirs, (RIGHT, LEFT))
                send_around(level, 1, 0)
                sweep_operator(0)
                root_copy.wait()
                for k in range(8):
                    p[k] = pr[block(k), :].T
                for rel in range(4):
                    from_sibling(level, 0, rel, mine)
                    keep_inner(level, rel, mine)
                keep_outer(level, 0)
                serve(level, 0, theirs, (1, 2))
                for rel in range(3):
                    from_sibling(level, 0, rel, theirs)
                    keep_inner(level, rel, theirs)
                serve(level, 0, theirs, (3,))
                from_sibling(level, 0, 3, theirs)
                keep_inner(level, 3, theirs)

        if level == LEVELS - 1:
            x = mm(pair(alpha), pair(beta))
            wf[0] = x
            keep(one, everything, x)
            serve(level, 1, mine)
            x = mm(pair(one), pair(one))
            wf[1] = x
            keep(two, everything, x)
            serve(level, 1, theirs)
            for rel in range(1, 4):
                keep_outer(level, rel)
            break

        own = rows_of(0)
        bit = next_bit(level, y)
        g = gathered[level][1]
        x = mm(
            [jnp.concatenate([alpha[i], alpha_out[i, own, :]], 0) for i in range(2)],
            pair(beta),
        )
        wf[0] = x[:IFACE]
        keep(one, everything, x[:IFACE])
        vf[:BLK, :] = x[IFACE:]
        for k in range(4):
            chosen, rest = g[y, 0, k // 2, k % 2], g[y, 1, k // 2, k % 2]
            vf[BLK:, block(k)] = -pick(bit, chosen, rest)
        keep(vs, everything, vf[...])
        x = mm([jnp.concatenate([one[i], vs[i]], 0) for i in range(2)], pair(one))
        wf[1] = x[:IFACE]
        keep(two, everything, x[:IFACE])
        x = vf[...] + x[IFACE:]
        vf[...] = x
        keep(vs, everything, x)
        (send_around if level == 0 else split_around)(level, 1, 1)
        x = vf[...] + mm(pair(vs), pair(two))
        vf[...] = x
        keep(vs, everything, x)
        keep(vs, everything, mm(pair(vs), pair(two)))
        serve(level, 1, 0)
        x = vf[...] + mm(pair(vs), pair(two))
        keep(ss.at[0], everything, x)
        x = -mm(pair(ss.at[0]), pair(alpha))
        keep(ss.at[1], slice(BLK, HALF), x[BLK:])
        for k in range(4):
            chosen, rest = g[y, 0, k // 2, k % 2], g[y, 1, k // 2, k % 2]
            keep(ss.at[1], slice(0, BLK), x[:BLK, block(k)] - pick(bit, rest, chosen), block(k))
        for rel in range(1, 4):
            from_sibling(level, 1, rel, 0)
        ext_copy(level).wait_recv()
        above = level + 1
        bit_y = bit_of(above, y)
        for kk in range(2):
            lower, upper = merged(level, kk, 0)
            gathered[above][0][y, own_map(above), c, kk] = pick(bit_y, upper, lower)
            outer = pick(bit_y, lower, upper)
            if above == LEVELS - 1:
                gathered[above][1][y, own_map(above), c, kk] = outer
            else:
                raw[above, own_map(above), kk] = outer

    for level in reversed(range(LEVELS)):
        alpha, beta, alpha_out, beta_out, coupling = (mats.at[level, i] for i in range(5))
        upper_half = own_map(level)
        for k in range(8):
            keep(fs, everything, p[k], block(k % 2 * 4 + k // 2))
        if level == LEVELS - 1:
            first, second = slice(0, IFACE), slice(IFACE, 2 * IFACE)
            x = mm((fs[0, :, first], fs[1, :, first]), pair(alpha_out))
            t32[0] = x
            keep(ts, everything, x)
            x = mm(pair(ts), pair(beta)) - mm((fs[0, :, second], fs[1, :, second]), pair(beta_out))
            keep(ds, everything, x)
            one, two = work.at[0], work.at[1]
            for factor in (one, two):
                x = x + mm(pair(ds), pair(factor))
                keep(ds, everything, x)
            keep(ds, everything, mm(pair(ds), pair(two)))
            x = x + mm(pair(ds), pair(two))
            t32[1] = x
            keep(ts, everything, x)
            x = mm(pair(ts), pair(alpha))
            t32[0] = pick(upper_half, -(t32[0] + x), t32[1])
        else:
            t32[0] = mm(pair(fs), pair(down.at[level]))
        for k in range(4):
            bit = bit_of(level, k)
            near = t32[0, :, block(k)]
            away = pick(upper_half, p[2 * k + 1], p[2 * k])
            even, odd = pick(bit, away, near), pick(bit, near, away)
            if level:
                p[2 * k] = even
                p[2 * k + 1] = odd
            else:
                out[0, block(2 * k), :] = even.T
                out[0, block(2 * k + 1), :] = odd.T

    for level in range(LEVELS):
        mine = own_map(level)
        for phase in range(2):
            whole = unit(level, phase, y, 0)
            parted = half(whole, 0)
            inner_top = level == LEVELS - 1 and not phase
            if level + phase:
                copy(level, phase, parted if inner_top else whole, ACROSS, left).wait_send()
            for index in range(SIBLING, BESIDE):
                copy(level, phase, whole, index, left).wait_send()
            if inner_top:
                for index in range(RIGHT, SIBLING):
                    copy(level, phase, parted, index, left).wait_send()
                for index in range(BESIDE + 2, COPIES):
                    copy(level, phase, parted, index, left).wait_send()
                copy(level, phase, parted, BESIDE + 1 - mine, left).wait_send()
            elif level == 1 and phase:
                sent(level, phase, 0, (RIGHT, LEFT, FAR))
                for rel in range(1, 4):
                    copy(level, phase, parted, BESIDE + 2 * rel + 1, left).wait_send()
                for index in (RIGHT, LEFT, FAR):
                    copy(level, phase, parted, index + 1, left).wait_send()
            elif level == 1:
                sent(level, 0, mine, (RIGHT, LEFT, FAR))
                sent(level, 0, 1 - mine, (FAR,))
            else:
                for u in range(2):
                    sent(level, phase, u, (RIGHT, LEFT, FAR))
    for level in range(2):
        ext_copy(level).wait_send()


def shards(leaf_maps, interface_blocks, root_data):
    vmem = pl.BlockSpec(memory_space=pltpu.VMEM)
    units = pltpu.VMEM((4, 2, 2, 2, BLK, BLK), F32)
    return pl.pallas_call(
        kernel,
        out_shape=jax.ShapeDtypeStruct((1,) + root_data.shape[1:], F32),
        in_specs=[
            pl.BlockSpec(memory_space=pltpu.SMEM),
            vmem,
            pl.BlockSpec(memory_space=pl.ANY),
        ],
        out_specs=vmem,
        scratch_shapes=[units] * 6
        + [
            pltpu.VMEM((LEVELS, 2, 2, BLK, BLK), F32),
            pltpu.VMEM((2, 2, BLK, BLK), F32),
            pltpu.VMEM((2, 2, 2 * IFACE, IFACE), BF16),
            pltpu.VMEM((LEVELS, 5, 2, IFACE, IFACE), BF16),
            pltpu.VMEM((4, 2, IFACE, IFACE), BF16),
            pltpu.VMEM((2, IFACE, IFACE), F32),
            pltpu.VMEM((2, HALF, IFACE), BF16),
            pltpu.VMEM((HALF, IFACE), F32),
            pltpu.VMEM((2, 2, HALF, IFACE), BF16),
            pltpu.VMEM((2, 2, 2, BLK, BLK), F32),
            pltpu.VMEM((2, 2, BLK, BLK), F32),
            pltpu.VMEM((2 * IFACE, BLK), F32),
            pltpu.VMEM((8, BLK, BLK), F32),
            pltpu.VMEM((2, BLK, 2 * IFACE), BF16),
            pltpu.VMEM((2, BLK, IFACE), F32),
            pltpu.VMEM((2, BLK, IFACE), BF16),
            pltpu.VMEM((2, BLK, IFACE), BF16),
            pltpu.SemaphoreType.DMA((LEVELS, 2, COPIES)),
            pltpu.SemaphoreType.DMA((LEVELS, 2, COPIES)),
            pltpu.SemaphoreType.DMA((2,)),
            pltpu.SemaphoreType.DMA((2,)),
            pltpu.SemaphoreType.DMA,
        ],
        compiler_params=pltpu.CompilerParams(
            collective_id=0, has_side_effects=True, vmem_limit_bytes=56 * 2**20
        ),
        name="merge_and_sweep",
    )(interface_blocks.transpose(0, 2, 1), leaf_maps, root_data)


def solution(mesh):
    return jax.shard_map(
        shards,
        mesh=mesh,
        in_specs=(P("box", None, "col"), P(), P(None, None, "col")),
        out_specs=P("box", None, "col"),
        check_vma=False,
    )
```

```python
import functools

import jax
import jax.numpy as jnp
from jax import lax
from jax.experimental import pallas as pl
from jax.experimental.pallas import tpu as pltpu
from jax.sharding import PartitionSpec as P

LEVELS = 3
IFACE = 512
BLK = 128
HALF = 256
F32 = jnp.float32
BF16 = jnp.bfloat16
MESH = pl.DeviceIdType.MESH

ACROSS, RIGHT, LEFT, FAR, SIBLING, BESIDE, COPIES = 0, 1, 3, 5, 7, 15, 23


def split(x):
    high = x.astype(BF16)
    return high, (x - high.astype(F32)).astype(BF16)


def mm(a, b):
    dot = functools.partial(jnp.dot, preferred_element_type=F32)
    return dot(a[0], b[0]) + (dot(a[0], b[1]) + dot(a[1], b[0]))


def mm_nt(a, b):
    dot = functools.partial(
        lax.dot_general, dimension_numbers=(((1,), (1,)), ((), ())), preferred_element_type=F32
    )
    return dot(a[0], b[0]) + (dot(a[0], b[1]) + dot(a[1], b[0]))


def pick(flag, yes, no):
    return jnp.where(jnp.broadcast_to(flag, yes.shape) == 1, yes, no)


def kernel(
    table, leaf, root, out,
    g0i, g0o, g1i, g1o, g2i, g2o,
    raw, both, down, mats, work, wf, vs, vf, ss, ext, dall, pr, p, fs, t32, ts, ds,
    send_sem, recv_sem, ext_send, ext_recv, root_sem,
):
    pos = lax.axis_index("box")
    y = lax.axis_index("col")
    c = pos % 2
    gathered = ((g0i, g0o), (g1i, g1o), (g2i, g2o))
    slots = (y, (y + 3) % 4, (y + 1) % 4, (y + 2) % 4)
    right, left, opposite, sibling = (pos, slots[2]), (pos, slots[1]), (pos, slots[3]), (pos ^ 1, y)

    root_copy = pltpu.make_async_copy(root.at[pos // 8], pr, root_sem)
    root_copy.start()

    barrier = pltpu.get_barrier_semaphore()
    for peer in (right, left, opposite, sibling, (pos ^ 2, y), (pos ^ 4, y)):
        pl.semaphore_signal(barrier, inc=1, device_id=peer, device_id_type=MESH)

    def own_map(level):
        return (pos >> level) & 1

    def bit_of(level, k):
        return table[level, k, pos - pos % 2**level] & 1

    def next_bit(level, k):
        return bit_of(level + 1, k) if level + 1 < LEVELS else jnp.int32(0)

    def unit(level, phase, slot, u):
        g = gathered[level][phase]
        return g.at[slot, c, u] if level + phase == 0 else g.at[slot, u, c]

    def copy(level, phase, ref, index, peer, src=None):
        return pltpu.make_async_remote_copy(
            src_ref=ref if src is None else src,
            dst_ref=ref,
            send_sem=send_sem.at[level, phase, index],
            recv_sem=recv_sem.at[level, phase, index],
            device_id=peer,
            device_id_type=MESH,
        )

    def send(*args):
        copy(*args).start()

    z_low = (pos >> 1) & 1
    beside = (pos ^ 2, y)

    def half(ref, which):
        return ref.at[which]

    def to_beside(level, phase, rel, u):
        ref = half(unit(level, phase, slots[rel], u), z_low)
        send(level, phase, ref, BESIDE + 2 * rel + u, beside)

    def split_around(level, phase, u):
        ref = half(unit(level, phase, y, u), z_low)
        send(level, phase, ref, RIGHT + u, right)
        send(level, phase, ref, LEFT + u, left)
        send(level, phase, ref, FAR + u, opposite)

    def serve_split(level, phase, u):
        for rel in (1, 2, 3):
            ref = half(unit(level, phase, slots[rel], u), z_low)
            copy(level, phase, ref, (0, RIGHT, LEFT, FAR)[rel] + u, left).wait_recv()
            to_beside(level, phase, rel, u)

    def join_split(level, phase, u, rels=(1, 2, 3)):
        for rel in rels:
            ref = half(unit(level, phase, slots[rel], u), 1 - z_low)
            copy(level, phase, ref, BESIDE + 2 * rel + u, beside).wait_recv()
            to_sibling(level, phase, rel, u)

    def to_sibling(level, phase, rel, u):
        send(level, phase, unit(level, phase, slots[rel], u), SIBLING + 2 * rel + u, sibling)

    def from_sibling(level, phase, rel, u):
        ref = unit(level, phase, slots[rel], u)
        copy(level, phase, ref, SIBLING + 2 * rel + u, sibling).wait_recv()

    def send_next(level, phase, u):
        ref = unit(level, phase, y, u)
        send(level, phase, ref, RIGHT + u, right)
        send(level, phase, ref, LEFT + u, left)

    def send_far(level, phase, u):
        send(level, phase, unit(level, phase, y, u), FAR + u, opposite)

    def send_around(level, phase, u):
        send_next(level, phase, u)
        send_far(level, phase, u)

    def sent(level, phase, u, kinds):
        ref = unit(level, phase, y, u)
        for index in kinds:
            copy(level, phase, ref, index + u, right).wait_send()

    def arrived(level, phase, rel, u):
        index = (0, RIGHT, LEFT, FAR)[rel] + u
        copy(level, phase, unit(level, phase, slots[rel], u), index, left).wait_recv()

    def relay_far(level):
        mine = own_map(level)
        ref = unit(level, 0, slots[3], mine)
        pltpu.make_async_remote_copy(
            src_ref=ref,
            dst_ref=ref,
            send_sem=send_sem.at[level, 0, FAR + 1 - mine],
            recv_sem=recv_sem.at[level, 0, FAR + mine],
            device_id=(pos ^ 2**level, y),
            device_id_type=MESH,
        ).start()

    def serve(level, phase, u, rels=(1, 2, 3)):
        for rel in rels:
            arrived(level, phase, rel, u)
            to_sibling(level, phase, rel, u)

    def rows_of(rel):
        return pl.ds(pl.multiple_of(slots[rel] * BLK, BLK), BLK)

    def block(k):
        return slice(k * BLK, (k + 1) * BLK)

    def keep(ref, rows, x, columns=slice(None)):
        high, low = split(x)
        ref[0, rows, columns] = high
        ref[1, rows, columns] = low

    def keep_inner(level, rel, m):
        for k in range(4):
            x = gathered[level][0][slots[rel], m, k // 2, k % 2]
            keep(mats.at[level, m], rows_of(rel), x, block(k))

    def keep_outer(level, rel, awaited=(0, 1)):
        for q in awaited:
            from_sibling(level, 1, rel, q)
        bit = next_bit(level, slots[rel])
        g = gathered[level][1]
        for k in range(4):
            chosen, rest = g[slots[rel], 0, k // 2, k % 2], g[slots[rel], 1, k // 2, k % 2]
            keep(mats.at[level, 2], rows_of(rel), pick(bit, rest, chosen), block(k))
            keep(mats.at[level, 3], rows_of(rel), pick(bit, chosen, rest), block(k))

    def pair(ref):
        return ref[0], ref[1]

    everything = slice(None)

    def order_outer(level):
        theirs = 1 - own_map(level)
        copy(level, 1, raw.at[level, theirs], ACROSS, sibling).wait_recv()
        bit = next_bit(level, y)
        g = gathered[level][1]
        g[y, 0, c] = pick(bit, raw[level, 1], raw[level, 0])
        g[y, 1, c] = pick(bit, raw[level, 0], raw[level, 1])
        to_sibling(level, 1, 0, 0)
        to_sibling(level, 1, 0, 1)

    def finish_cubes(level):
        one, two, four, three = (work.at[i] for i in range(4))
        x = mm(pair(one), pair(two)) + wf[0] + wf[1]
        row = lax.broadcasted_iota(jnp.int32, x.shape, 0)
        column = lax.broadcasted_iota(jnp.int32, x.shape, 1)
        x = x + jnp.where(row == column, 1.0, 0.0)
        wf[0] = x
        keep(three, everything, x)
        keep(four, everything, mm(pair(two), pair(two)))

    def finish_coupling(level):
        keep(mats.at[level, 4], everything, wf[0] + mm(pair(work.at[3]), pair(work.at[2])))

    def sweep_operator(level):
        alpha, beta, alpha_out, beta_out, coupling = (mats.at[level, i] for i in range(5))
        x = mm(pair(alpha_out), pair(beta))
        keep(work.at[0], everything, x)
        keep(down.at[level], slice(0, IFACE), mm(pair(work.at[0]), pair(coupling)))
        keep(down.at[level], slice(IFACE, 2 * IFACE), -mm(pair(beta_out), pair(coupling)))

    def sweep_operator_beta(level):
        upper_half = own_map(level)
        for i in range(2):
            rows = slice(i * IFACE, (i + 1) * IFACE)
            near = (down[level, 0, rows, :], down[level, 1, rows, :])
            x = -mm(near, pair(mats.at[level, 0]))
            if i == 0:
                x = x - (mats[level, 2, 0].astype(F32) + mats[level, 2, 1].astype(F32))
            held = near[0].astype(F32) + near[1].astype(F32)
            keep(down.at[level], rows, pick(upper_half, x, held))

    def ext_copy(level):
        return pltpu.make_async_remote_copy(
            src_ref=dall.at[1 - c] if level == 0 else ext.at[1, own_map(1)],
            dst_ref=ext.at[level, own_map(level)],
            send_sem=ext_send.at[level],
            recv_sem=ext_recv.at[level],
            device_id=(pos ^ 2**level, y),
            device_id_type=MESH,
        )

    def merged(level, kk, rest):
        k = 2 * c + kk
        bit = bit_of(level + 1, k)
        part = 1 - bit if rest else bit
        g = gathered[level][1]
        r = split(jnp.concatenate([g[k, rest, i // 2, i % 2] for i in range(4)], 1))
        x = mm_nt((ss[part, 0], ss[part, 1]), r)
        kept = pick(part, ext[level, 1, kk], ext[level, 0, kk])
        lower = x[:BLK] + pick(part, jnp.zeros_like(kept), kept)
        upper = x[BLK:] + pick(part, kept, jnp.zeros_like(kept))
        return lower, upper

    bit_y = bit_of(0, y)
    for k in range(4):
        bit = bit_of(0, k)
        even = leaf[0, 2 * k * BLK : (2 * k + 1) * BLK, :]
        odd = leaf[0, (2 * k + 1) * BLK : (2 * k + 2) * BLK, :]
        near = pick(bit, odd, even).T
        away = pick(bit, even, odd).T
        g0i[y, c, k // 2, k % 2] = pick(bit_y, near[BLK:], near[:BLK])
        both[k // 2, k % 2] = pick(bit_y, near[:BLK], near[BLK:])
        dall[k // 2, k % 2] = pick(bit_y, away[:BLK], away[BLK:])

    pl.semaphore_wait(barrier, 6)

    for level in range(LEVELS):
        alpha, beta, alpha_out, beta_out, coupling = (mats.at[level, i] for i in range(5))
        one, two, four, three = (work.at[i] for i in range(4))
        mine = own_map(level)
        if level == 0:
            first, second = unit(0, 0, y, 0), unit(0, 0, y, 1)
            send(0, 0, first, RIGHT, right)
            send(0, 0, second, LEFT + 1, left)
            send(0, 0, second, RIGHT + 1, right)
            send(0, 0, first, LEFT, left)
            to_sibling(0, 0, 0, 0)
            to_sibling(0, 0, 0, 1)
            send(0, 1, raw.at[0, mine], ACROSS, sibling, both.at[1 - c])
            ext_copy(0).start()
            raw[0, mine] = both[c]
            ext[0, mine] = dall[c]
            order_outer(0)
            for u in range(2):
                from_sibling(0, 0, 0, u)
            keep_inner(0, 0, 0)
            keep_inner(0, 0, 1)
            arrived(0, 0, 1, 0)
            send(0, 0, unit(0, 0, slots[1], 0), FAR, right)
            to_sibling(0, 0, 1, 0)
            arrived(0, 0, 2, 1)
            send(0, 0, unit(0, 0, slots[2], 1), FAR + 1, left)
            to_sibling(0, 0, 2, 1)
            keep_outer(0, 0)
            arrived(0, 0, 1, 1)
            to_sibling(0, 0, 1, 1)
            arrived(0, 0, 2, 0)
            to_sibling(0, 0, 2, 0)
            send_around(0, 1, 0)
            for rel in (1, 2):
                for u in range(2):
                    from_sibling(0, 0, rel, u)
                keep_inner(0, rel, 0)
                keep_inner(0, rel, 1)
            for u in range(2):
                arrived(0, 0, 3, u)
                to_sibling(0, 0, 3, u)
            for u in range(2):
                from_sibling(0, 0, 3, u)
            keep_inner(0, 3, 0)
            keep_inner(0, 3, 1)
        else:
            theirs = 1 - mine
            last = level == LEVELS - 1
            partner = (pos ^ 2**level, y)
            if last:
                send(level, 0, half(unit(level, 0, y, mine), z_low), ACROSS, partner)
                split_around(level, 0, mine)
                to_sibling(level, 0, 0, mine)
                send(level, 1, unit(level, 1, y, mine), ACROSS, partner)
                to_sibling(level, 1, 0, mine)
                finish_cubes(level - 1)
                serve_split(level - 1, 1, 1)
                send_next(level, 1, mine)
                sweep_operator_beta(0)
                finish_coupling(level - 1)
                ref = half(unit(level, 0, y, theirs), z_low)
                copy(level, 0, ref, ACROSS, partner).wait_recv()
                split_around(level, 0, theirs)
                to_beside(level, 0, 0, theirs)
                serve_split(level, 0, mine)
                join_split(level - 1, 1, 1)
                join_split(level, 0, theirs, (0,))
                for rel in range(1, 4):
                    keep_outer(level - 1, rel, (1,))
                send_far(level, 1, mine)
                join_split(level, 0, mine)
                serve_split(level, 0, theirs)
                copy(level, 1, unit(level, 1, y, theirs), ACROSS, partner).wait_recv()
                to_sibling(level, 1, 0, theirs)
                send_around(level, 1, theirs)
                sweep_operator(1)
                for rel in range(4):
                    from_sibling(level, 0, rel, mine)
                    keep_inner(level, rel, mine)
                keep_outer(level, 0)
                for rel in range(4):
                    if rel:
                        join_split(level, 0, theirs, (rel,))
                    if rel > 1:
                        from_sibling(level, 0, rel - 1, theirs)
                        keep_inner(level, rel - 1, theirs)
                    elif rel == 1:
                        from_sibling(level, 0, 0, theirs)
                        keep_inner(level, 0, theirs)
                from_sibling(level, 0, 3, theirs)
                keep_inner(level, 3, theirs)
            else:
                send(level, 0, unit(level, 0, y, mine), ACROSS, partner)
                send_around(level, 0, mine)
                to_sibling(level, 0, 0, mine)
                send(level, 1, raw.at[level, mine], ACROSS, partner)
                finish_cubes(level - 1)
                copy(level, 0, unit(level, 0, y, theirs), ACROSS, partner).wait_recv()
                send_next(level, 0, theirs)
                to_sibling(level, 0, 0, theirs)
                serve(level - 1, 1, 1)
                order_outer(level)
                finish_coupling(level - 1)
                serve(level, 0, mine)
                relay_far(level)
                for rel in range(1, 4):
                    keep_outer(level - 1, rel, (1,))
                bit_y = bit_of(1, y)
                for kk in range(2):
                    lower, upper = merged(0, kk, 1)
                    ext[1, mine, kk] = pick(bit_y, lower, upper)
                ext_copy(1).start()
                sent(level, 0, theirs, (RIGHT, LEFT))
                send_around(level, 1, 0)
                serve(level, 0, theirs, (1, 2))
                sweep_operator(0)
                root_copy.wait()
                for k in range(8):
                    p[k] = pr[block(k), :].T
                for rel in range(4):
                    from_sibling(level, 0, rel, mine)
                    keep_inner(level, rel, mine)
                keep_outer(level, 0)
                for rel in range(3):
                    from_sibling(level, 0, rel, theirs)
                    keep_inner(level, rel, theirs)
                serve(level, 0, theirs, (3,))
                from_sibling(level, 0, 3, theirs)
                keep_inner(level, 3, theirs)

        if level == LEVELS - 1:
            x = mm(pair(alpha), pair(beta))
            wf[0] = x
            keep(one, everything, x)
            serve(level, 1, mine)
            x = mm(pair(one), pair(one))
            wf[1] = x
            keep(two, everything, x)
            serve(level, 1, theirs)
            for rel in range(1, 4):
                keep_outer(level, rel)
            break

        own = rows_of(0)
        bit = next_bit(level, y)
        g = gathered[level][1]
        x = mm(
            [jnp.concatenate([alpha[i], alpha_out[i, own, :]], 0) for i in range(2)],
            pair(beta),
        )
        wf[0] = x[:IFACE]
        keep(one, everything, x[:IFACE])
        vf[:BLK, :] = x[IFACE:]
        for k in range(4):
            chosen, rest = g[y, 0, k // 2, k % 2], g[y, 1, k // 2, k % 2]
            vf[BLK:, block(k)] = -pick(bit, chosen, rest)
        keep(vs, everything, vf[...])
        x = mm([jnp.concatenate([one[i], vs[i]], 0) for i in range(2)], pair(one))
        wf[1] = x[:IFACE]
        keep(two, everything, x[:IFACE])
        x = vf[...] + x[IFACE:]
        vf[...] = x
        keep(vs, everything, x)
        (send_around if level == 0 else split_around)(level, 1, 1)
        x = vf[...] + mm(pair(vs), pair(two))
        vf[...] = x
        keep(vs, everything, x)
        keep(vs, everything, mm(pair(vs), pair(two)))
        serve(level, 1, 0)
        x = vf[...] + mm(pair(vs), pair(two))
        keep(ss.at[0], everything, x)
        x = -mm(pair(ss.at[0]), pair(alpha))
        keep(ss.at[1], slice(BLK, HALF), x[BLK:])
        for k in range(4):
            chosen, rest = g[y, 0, k // 2, k % 2], g[y, 1, k // 2, k % 2]
            keep(ss.at[1], slice(0, BLK), x[:BLK, block(k)] - pick(bit, rest, chosen), block(k))
        for rel in range(1, 4):
            from_sibling(level, 1, rel, 0)
        ext_copy(level).wait_recv()
        above = level + 1
        bit_y = bit_of(above, y)
        for kk in range(2):
            lower, upper = merged(level, kk, 0)
            gathered[above][0][y, own_map(above), c, kk] = pick(bit_y, upper, lower)
            outer = pick(bit_y, lower, upper)
            if above == LEVELS - 1:
                gathered[above][1][y, own_map(above), c, kk] = outer
            else:
                raw[above, own_map(above), kk] = outer

    for level in reversed(range(LEVELS)):
        alpha, beta, alpha_out, beta_out, coupling = (mats.at[level, i] for i in range(5))
        upper_half = own_map(level)
        for k in range(8):
            keep(fs, everything, p[k], block(k % 2 * 4 + k // 2))
        if level == LEVELS - 1:
            first, second = slice(0, IFACE), slice(IFACE, 2 * IFACE)
            x = mm((fs[0, :, first], fs[1, :, first]), pair(alpha_out))
            t32[0] = x
            keep(ts, everything, x)
            x = mm(pair(ts), pair(beta)) - mm((fs[0, :, second], fs[1, :, second]), pair(beta_out))
            keep(ds, everything, x)
            one, two = work.at[0], work.at[1]
            for factor in (one, two):
                x = x + mm(pair(ds), pair(factor))
                keep(ds, everything, x)
            keep(ds, everything, mm(pair(ds), pair(two)))
            x = x + mm(pair(ds), pair(two))
            t32[1] = x
            keep(ts, everything, x)
            x = mm(pair(ts), pair(alpha))
            t32[0] = pick(upper_half, -(t32[0] + x), t32[1])
        else:
            x = mm(pair(fs), pair(down.at[level]))
            if level:
                keep(ts, everything, x)
                through = mm((fs[0, :, :IFACE], fs[1, :, :IFACE]), pair(alpha_out))
                x = pick(upper_half, -(through + mm(pair(ts), pair(alpha))), x)
            t32[0] = x
        for k in range(4):
            bit = bit_of(level, k)
            near = t32[0, :, block(k)]
            away = pick(upper_half, p[2 * k + 1], p[2 * k])
            even, odd = pick(bit, away, near), pick(bit, near, away)
            if level:
                p[2 * k] = even
                p[2 * k + 1] = odd
            else:
                out[0, block(2 * k), :] = even.T
                out[0, block(2 * k + 1), :] = odd.T

    for level in range(LEVELS):
        mine = own_map(level)
        for phase in range(2):
            whole = unit(level, phase, y, 0)
            parted = half(whole, 0)
            inner_top = level == LEVELS - 1 and not phase
            if level + phase:
                copy(level, phase, parted if inner_top else whole, ACROSS, left).wait_send()
            for index in range(SIBLING, BESIDE):
                copy(level, phase, whole, index, left).wait_send()
            if inner_top:
                for index in range(RIGHT, SIBLING):
                    copy(level, phase, parted, index, left).wait_send()
                for index in range(BESIDE + 2, COPIES):
                    copy(level, phase, parted, index, left).wait_send()
                copy(level, phase, parted, BESIDE + 1 - mine, left).wait_send()
            elif level == 1 and phase:
                sent(level, phase, 0, (RIGHT, LEFT, FAR))
                for rel in range(1, 4):
                    copy(level, phase, parted, BESIDE + 2 * rel + 1, left).wait_send()
                for index in (RIGHT, LEFT, FAR):
                    copy(level, phase, parted, index + 1, left).wait_send()
            elif level == 1:
                sent(level, 0, mine, (RIGHT, LEFT, FAR))
                sent(level, 0, 1 - mine, (FAR,))
            else:
                for u in range(2):
                    sent(level, phase, u, (RIGHT, LEFT, FAR))
    for level in range(2):
        ext_copy(level).wait_send()


def shards(leaf_maps, interface_blocks, root_data):
    vmem = pl.BlockSpec(memory_space=pltpu.VMEM)
    units = pltpu.VMEM((4, 2, 2, 2, BLK, BLK), F32)
    return pl.pallas_call(
        kernel,
        out_shape=jax.ShapeDtypeStruct((1,) + root_data.shape[1:], F32),
        in_specs=[
            pl.BlockSpec(memory_space=pltpu.SMEM),
            vmem,
            pl.BlockSpec(memory_space=pl.ANY),
        ],
        out_specs=vmem,
        scratch_shapes=[units] * 6
        + [
            pltpu.VMEM((LEVELS, 2, 2, BLK, BLK), F32),
            pltpu.VMEM((2, 2, BLK, BLK), F32),
            pltpu.VMEM((2, 2, 2 * IFACE, IFACE), BF16),
            pltpu.VMEM((LEVELS, 5, 2, IFACE, IFACE), BF16),
            pltpu.VMEM((4, 2, IFACE, IFACE), BF16),
            pltpu.VMEM((2, IFACE, IFACE), F32),
            pltpu.VMEM((2, HALF, IFACE), BF16),
            pltpu.VMEM((HALF, IFACE), F32),
            pltpu.VMEM((2, 2, HALF, IFACE), BF16),
            pltpu.VMEM((2, 2, 2, BLK, BLK), F32),
            pltpu.VMEM((2, 2, BLK, BLK), F32),
            pltpu.VMEM((2 * IFACE, BLK), F32),
            pltpu.VMEM((8, BLK, BLK), F32),
            pltpu.VMEM((2, BLK, 2 * IFACE), BF16),
            pltpu.VMEM((2, BLK, IFACE), F32),
            pltpu.VMEM((2, BLK, IFACE), BF16),
            pltpu.VMEM((2, BLK, IFACE), BF16),
            pltpu.SemaphoreType.DMA((LEVELS, 2, COPIES)),
            pltpu.SemaphoreType.DMA((LEVELS, 2, COPIES)),
            pltpu.SemaphoreType.DMA((2,)),
            pltpu.SemaphoreType.DMA((2,)),
            pltpu.SemaphoreType.DMA,
        ],
        compiler_params=pltpu.CompilerParams(
            collective_id=0, has_side_effects=True, vmem_limit_bytes=56 * 2**20
        ),
        name="merge_and_sweep",
    )(interface_blocks.transpose(0, 2, 1), leaf_maps, root_data)


def solution(mesh):
    return jax.shard_map(
        shards,
        mesh=mesh,
        in_specs=(P("box", None, "col"), P(), P(None, None, "col")),
        out_specs=P("box", None, "col"),
        check_vma=False,
    )
```
